256 devices in a mesh: shard: 64 (over z, y, core), rep: 4 (over x).
Axes of the slice: x: 4, y: 4, z: 8, core: 2. Of those that a mesh axis runs over, the one named last changes fastest.
Arguments:
- table: bfloat16 [2048, 1024], P('shard'), may hold values from -6 to 6
- self_feat: bfloat16 [2048, 1024], P(('shard', 'rep')), may hold values from -24 to 24
- weight: bfloat16 [2048, 1024], replicated, may hold values from -0.125 to 0.125
- owners: int32 [2048, 67, 1], P(('shard', 'rep')), may hold values from 0 to 63; in each aligned block of 536 rows (0 to 535, 536 to 1071, ..., all dimensions but the last counted through in order) at most 17 rows name the same one
- item_rows: int32 [2048, 67], P(('shard', 'rep')), may hold values from 0 to 31
- importance: int32 [2048, 50], P(('shard', 'rep')), may hold values from 1 to 32
Outputs:
- grad_self: float32 [2048, 1024], P(('shard', 'rep'))
- grad_weight: float32 [2048, 1024], P(('shard', 'rep'))
- grad_table: float32 [2048, 1024], P(('shard', 'rep'))
The draws below stay inside these ranges and needn't reach their ends.
Inputs may be any that keep to these rules, and one draw needn't show every extreme that they name: `owners`: among the 536 requests of the queries of one device, no owner is named more than 17 times, and in some device's queries one owner is named exactly 17 times.
All inputs are finite; a program needn't handle non-finite values.
Results may differ from the reference program's by a relative error of at most 0.0095.
Values may be sent and summed in bfloat16 or wider, within the bound.
A program may use at most 64 MiB of HBM per device.

```python
import math
import jax
import jax.numpy as jnp
import numpy as np
from jax import lax

F = 1024
K = 50
QDEV = 8
ITEMS_DEV = 32
SLOTS = 67
CAP = 17
BATCH = 2048
ITEMS = 2048
N_SHARD = 64


def with_ends(drawn, rng, low, top_value):
    extent = drawn.shape
    index_at = [jax.random.randint(jax.random.fold_in(rng, axis), (), 0, extent[axis]) for axis in range(len(extent))]
    drawn = drawn.at[tuple(index_at)].set(low)
    longest = extent.index(max(extent))
    index_at[longest] = (index_at[longest] + 1) % extent[longest]
    return drawn.at[tuple(index_at)].set(top_value)


def with_spikes(result, own_key, source, target, parts, factor):
    def block_of(axis_at):
        return (jnp.arange(result.shape[axis_at]) // (result.shape[axis_at] // parts)).reshape((-1,) + (1,) * (result.ndim - 1 - axis_at))

    first = jax.random.permutation(own_key, parts)[block_of(target)]
    second = (block_of(target) + parts // 2) % parts
    return jnp.where((block_of(source) == first) | (block_of(source) == second), factor * result, result)


def steps_of(rng, extent, split, low, top_value):
    def one(dim, shards_of):
        draws = jax.random.uniform(jax.random.fold_in(jax.random.fold_in(rng, 6), dim), (shards_of,), jnp.float32, low / len(split), top_value / len(split))
        return jnp.repeat(jnp.exp(draws), extent[dim] // shards_of).reshape((-1,) + (1,) * (len(extent) - dim - 1))

    gain = one(*split[0])
    for cut in split[1:]:
        gain = gain * one(*cut)
    return gain


def routed_block(stream_key, own, number, rows, number_of, top, bound, lean):
    sequence = jax.random.permutation(stream_key, number_of)
    heavy_load, usual = portions_of(number_of, rows * top, bound, lean, True), portions_of(number_of, rows * top, bound, lean, False)
    places = jnp.arange(number_of)

    def named(sizes, rotation):
        used = int((sizes > 0).sum())
        fixed = max(1, used // 4)
        shifted = fixed + (places - fixed + rotation * (used - fixed)) % max(1, number_of - fixed)
        return jnp.zeros((number_of,), jnp.int32).at[sequence[jnp.where(places < fixed, places, shifted)]].set(jnp.asarray(sizes, jnp.int32))

    sizes = jnp.where(number % 4 == 0, named(heavy_load, number // 4), named(usual, number - number // 4 - 1))
    mixed = jax.random.permutation(jax.random.fold_in(own, 3), number_of)
    giver, taker = mixed[0:number_of // 2 * 2:2], mixed[1:number_of // 2 * 2:2]
    margin = jnp.minimum(sizes[giver] - 1, bound - sizes[taker]) // 2
    margin = jnp.where((giver == sequence[0]) | (taker == sequence[0]) | (sizes[taker] == 0), 0, jnp.maximum(margin, 0))
    shifted = jax.random.randint(jax.random.fold_in(own, 4), (number_of // 2,), 0, 1 << 20) % (margin + 1)
    sizes = sizes.at[giver].add(-shifted).at[taker].add(shifted)
    labels = jnp.searchsorted(jnp.cumsum(sizes), jnp.arange(rows * top), side="right").astype(jnp.int32)
    table = labels.reshape(top, rows).T
    table = table[jax.random.permutation(jax.random.fold_in(own, 1), rows)]
    rotation = jax.random.randint(jax.random.fold_in(own, 2), (rows, 1), 0, top)
    return jnp.take_along_axis(table, (jnp.arange(top)[None, :] + rotation) % top, axis=1)


def portions_of(amount, total, reach, skew, full):
    loads = [(1 << 20) // math.isqrt(rank ** skew) + 1 for rank in range(1, amount + 1)]
    largest = reach if full else min(reach, max(-(-total // amount), total * loads[0] // sum(loads)))
    least = 1 if total - largest >= amount - 1 else 0
    counts, surplus = [largest] + [least] * (amount - 1), total - largest - least * (amount - 1)
    while surplus > 0:
        free = [i for i in range(1, amount) if counts[i] < largest] or [i for i in range(1, amount) if counts[i] < reach]
        whole, remaining = sum([loads[i] for i in free]), surplus
        for i in free:
            more = min(reach - counts[i], max(1, remaining * loads[i] // whole), surplus)
            counts[i] = counts[i] + more
            surplus = surplus - more
    return np.array(counts)


def noise(own_key, dims, deviation, bound, cuts=(), kind=jnp.bfloat16):
    gain = steps_of(own_key, dims, cuts, -0.22, 0.18) if cuts else 1.0
    drawn = jax.random.normal(own_key, dims, jnp.float32) * deviation * gain
    return jnp.minimum(jnp.maximum(drawn, -bound), bound).astype(kind)


def heavy_noise(key, shape, scale, most, pieces, heavy, held_as=jnp.bfloat16):
    values = scale * jax.random.normal(key, shape, jnp.float32)
    if pieces:
        values = values * steps_of(key, shape, pieces, -0.22, 0.18)
    return jnp.clip(with_spikes(values, jax.random.fold_in(key, 3), *heavy), -most, most).astype(held_as)


def setup_inputs(seed: int = 0) -> dict:
    key_list = jax.random.split(jax.random.key(seed), 7)
    table = noise(key_list[0], (ITEMS, F), 1.0, 6.0, ((0, 64),))
    self_feat = heavy_noise(key_list[1], (BATCH, F), 1.0, 24.0, ((0, 256),), (0, 1, 256, 6.0))
    weight = noise(key_list[2], (2 * F, F), (2 * F) ** -0.5, 0.125)
    owners_keys = jax.random.split(jax.random.fold_in(key_list[3], 1), BATCH * SLOTS // (QDEV * SLOTS))
    owners_turns = jax.random.permutation(jax.random.fold_in(key_list[3], 3), BATCH * SLOTS // (QDEV * SLOTS))
    owners = jax.vmap(lambda own, number: routed_block(jax.random.fold_in(key_list[3], 2), own, number, QDEV * SLOTS, N_SHARD, 1, CAP, 2))(owners_keys, owners_turns).reshape((BATCH, SLOTS, 1))
    item_rows = with_ends(jax.random.randint(key_list[4], (BATCH, SLOTS), 0, ITEMS_DEV), jax.random.fold_in(key_list[4], 1), 0, ITEMS_DEV - 1).astype(jnp.int32)
    importance = with_ends(jax.random.randint(key_list[5], (BATCH, K), 1, 33), jax.random.fold_in(key_list[5], 1), 1, 32).astype(jnp.int32)
    return {"table": table, "self_feat": self_feat, "weight": weight, "owners": owners, "item_rows": item_rows, "importance": importance}


MARGIN = 0.5
eps = 1e-06

def forward_backward(fetched, self_feat, weight, importance):
    neighbours = fetched[:, :K].astype(jnp.float32)
    weights_f = importance.astype(jnp.float32)
    shares = weights_f / lax.optimization_barrier(jnp.sum(weights_f, axis=1, keepdims=True))
    pooled = jnp.einsum('qk,qkf->qf', shares, neighbours).astype(jnp.bfloat16)
    joined = jnp.concatenate([self_feat, pooled], axis=1)
    preact = jnp.dot(joined, weight, preferred_element_type=jnp.float32)
    gate_value = jax.nn.sigmoid(preact)
    activation = preact * gate_value
    act_norm = jnp.sqrt(lax.optimization_barrier(jnp.sum(activation * activation, axis=1, keepdims=True)) + eps)
    unit_vec = activation / act_norm
    candidates = fetched[:, K:].astype(jnp.float32)
    scores = jnp.einsum('qf,qcf->qc', unit_vec, candidates)
    slopes = jax.nn.sigmoid(scores[:, 1:] - scores[:, :1] + MARGIN)
    slope_sum = lax.optimization_barrier(jnp.sum(slopes, axis=1, keepdims=True))
    grad_unit = jnp.einsum('qn,qnf->qf', slopes, candidates[:, 1:]) - slope_sum * candidates[:, 0]
    grad_act = (grad_unit - unit_vec * lax.optimization_barrier(jnp.sum(unit_vec * grad_unit, axis=1, keepdims=True))) / act_norm
    grad_pre = (grad_act * gate_value * (1.0 + preact * (1.0 - gate_value))).astype(jnp.bfloat16)
    grad_weight = jnp.dot(joined.T, grad_pre, preferred_element_type=jnp.float32)
    grad_joined = jnp.dot(grad_pre, weight.T, preferred_element_type=jnp.float32)
    feat_dim = self_feat.shape[1]
    grad_self = grad_joined[:, :feat_dim]
    grad_neigh = shares[:, :, None] * grad_joined[:, None, feat_dim:]
    grad_pos = -slope_sum[:, :, None] * unit_vec[:, None, :]
    grad_neg = slopes[:, :, None] * unit_vec[:, None, :]
    row_terms = jnp.concatenate([grad_neigh, grad_pos, grad_neg], axis=1).astype(jnp.bfloat16)
    return (grad_self, grad_weight, row_terms)

def reference(table, self_feat, weight, owners, item_rows, importance):
    item_ids = (owners[:, :, 0] * ITEMS_DEV + item_rows).astype(jnp.int32)
    block_count = BATCH // QDEV

    def one_block(totals_pair, block_index):
        table_grad, weight_grad = totals_pair
        first_query = (block_index * QDEV).astype(jnp.int32)
        ids_block = lax.dynamic_slice_in_dim(item_ids, first_query, QDEV, 0)
        self_block = lax.dynamic_slice_in_dim(self_feat, first_query, QDEV, 0)
        weight_block = lax.dynamic_slice_in_dim(importance, first_query, QDEV, 0)
        fetched = table[ids_block]
        grad_self, grad_part, row_terms = forward_backward(fetched, self_block, weight, weight_block)
        table_grad = table_grad.at[ids_block.reshape(-1)].add(row_terms.reshape(-1, F).astype(jnp.float32))
        return ((table_grad, weight_grad + grad_part), grad_self)
    start_pair = (jnp.zeros((ITEMS, F), jnp.float32), jnp.zeros((2 * F, F), jnp.float32))
    final_pair, stacked = lax.scan(one_block, start_pair, jnp.arange(block_count, dtype=jnp.int32))
    return (stacked.reshape(BATCH, F), final_pair[1], final_pair[0])
```

```python
import jax
import jax.numpy as jnp
from jax import lax
from jax.experimental import pallas as pl
from jax.experimental.pallas import tpu as pltpu
from jax.sharding import PartitionSpec as P

MESH = pl.DeviceIdType.MESH
MARGIN = 0.5
EPS = 1e-06
K = 50
C = 17
NZ, NY, NX = 8, 4, 4
NB = NZ * NY
NE = NY * NX
Q = 8
G = NZ * Q
L = 128
ITEMS = 2048
HALF = ITEMS // 2
F32, BF16 = jnp.float32, jnp.bfloat16
QI_, SF_, TA_, TP_, PO_, PC_, GP_, HW_, HT_, EW_, ET_, OW_, OT_ = range(13)


def tdot(a, b):
    return lax.dot_general(a, b, (((0,), (0,)), ((), ())), preferred_element_type=F32)


def ntdot(a, b):
    return lax.dot_general(a, b, (((1,), (1,)), ((), ())), preferred_element_type=F32)


def kernel(
    tab, sf, qin, w_hbm, o_self, o_w, o_t,
    t_all, qi, sf_all, pooled, parts, gpre, hot, id_b, imp_b, w_b, cand, w2,
    wf, wbp, wtop, rw, rt, hws, hwr, hts, htr, esw, est, eww, ewt, rsw, rst, oww, owt, gself,
    sems, wsem,
):
    s = lax.axis_index("shard")
    x = lax.axis_index("rep")
    c = lax.rem(s, 2)
    b = lax.div(s, 2)
    z = lax.div(b, NY)
    y = lax.rem(b, NY)
    e = y * NX + x
    partner = (b * 2 + 1 - c, x)

    def on_plane(off):
        other = lax.rem(b + off, NB)
        return other, (other * 2 + c, x)

    def on_line(off):
        other = lax.rem(z + off, NZ)
        return other, ((other * NY + y) * 2 + c, x)

    def on_face(off):
        other = lax.rem(e + off, NE)
        return other, ((z * NY + lax.div(other, NX)) * 2 + c, lax.rem(other, NX))

    def send(src, dst, row, to):
        pltpu.make_async_remote_copy(
            src_ref=src, dst_ref=dst, send_sem=sems.at[row, 0], recv_sem=sems.at[row, 1],
            device_id=to, device_id_type=MESH,
        ).start()

    def done(ref, row):
        return pltpu.make_async_remote_copy(
            src_ref=ref, dst_ref=ref, send_sem=sems.at[row, 0], recv_sem=sems.at[row, 1],
            device_id=partner, device_id_type=MESH,
        )

    def each(n, body):
        def step(i, carry):
            body(i)
            return carry
        lax.fori_loop(1, n, step, 0)

    zcol = pl.ds(pl.multiple_of(z * L, L), L)
    zrow = pl.ds(pl.multiple_of(z * L, L), L)
    loads = [
        pltpu.make_async_copy(w_hbm.at[:, zcol], wf, wsem.at[0]),
        pltpu.make_async_copy(
            w_hbm.at[pl.ds(pl.multiple_of(1024 + z * L, L), L), :], wbp, wsem.at[1]),
        pltpu.make_async_copy(w_hbm.at[pl.ds(0, 1024), :], wtop, wsem.at[2]),
    ]
    for load in loads:
        load.start()

    bar = pltpu.get_barrier_semaphore()

    def greet(to):
        pl.semaphore_signal(bar, inc=1, device_id=to, device_id_type=MESH)

    each(NB, lambda i: greet(on_plane(i)[1]))
    each(NE, lambda i: greet(on_face(i)[1]))
    greet(partner)
    qi[z] = qin[...]
    own_self = sf[...].astype(F32)
    sf_all[z] = jnp.concatenate([own_self[:, :512], own_self[:, 512:]], axis=0).astype(BF16)
    t_all[c, b] = tab[:, zcol]
    pl.semaphore_wait(bar, NB - 1 + NE - 1 + 1)

    each(NZ, lambda i: send(qi.at[z], qi.at[z], QI_, on_line(i)[1]))

    def send_table(i):
        other, to = on_plane(i)
        cols = pl.ds(pl.multiple_of(lax.div(other, NY) * L, L), L)
        send(tab.at[:, cols], t_all.at[c, b], TA_, to)

    each(NB, send_table)
    each(NZ, lambda i: send(sf_all.at[z], sf_all.at[z], SF_, on_line(i)[1]))

    done(qi.at[pl.ds(0, NZ - 1)], QI_).wait_recv()
    ids = qi[:, 0:Q, :].reshape(G, L)
    imp = qi[:, Q:2 * Q, :].reshape(G, L).astype(F32)
    for k in range(K + C):
        id_b[k] = jnp.broadcast_to(ids[:, k:k + 1], (G, L))
    for k in range(K):
        imp_b[k] = jnp.broadcast_to(imp[:, k:k + 1], (G, L))
    inv = 1.0 / jnp.sum(imp, axis=1, keepdims=True)
    lane = lax.broadcasted_iota(jnp.int32, (G, L), 1)

    def hot_chunk(h, carry):
        here = lane + h * L
        cols = pl.ds(pl.multiple_of(h * L, L), L)

        def add(k, acc):
            return acc + jnp.where(id_b[k] == here, imp_b[k], 0.0)

        acc = lax.fori_loop(0, K, add, jnp.zeros((G, L), F32), unroll=10)
        hot[0, :, cols] = acc.astype(BF16)
        for k in range(C):
            hot[1 + k, :, cols] = jnp.where(id_b[K + k] == here, 1.0, 0.0).astype(BF16)
        return carry

    lax.fori_loop(0, ITEMS // L, hot_chunk, 0)

    loads[0].wait()
    done(sf_all.at[pl.ds(0, NZ - 1)], SF_).wait_recv()
    self2 = sf_all[...].reshape(2 * G, 512)
    w_self = jnp.concatenate([wf[0:512, :], wf[512:1024, :]], axis=1)
    pre2 = jnp.dot(self2, w_self, preferred_element_type=F32).reshape(NZ, 2, Q, 2 * L)
    pre_self = (pre2[:, 0, :, :L] + pre2[:, 1, :, L:]).reshape(G, L)

    done(t_all.at[c, pl.ds(0, NB - 1)], TA_).wait_recv()
    send(t_all.at[c], t_all.at[c], TP_, partner)
    done(t_all.at[1 - c], TP_).wait_recv()

    rows = t_all[...].reshape(ITEMS, L)
    mine = jnp.dot(hot[0], rows, preferred_element_type=F32) * inv
    pooled[z] = mine.astype(BF16)
    each(NZ, lambda i: send(pooled.at[z], pooled.at[z], PO_, on_line(i)[1]))
    cand[...] = jnp.dot(
        hot[1:1 + C].reshape(C * G, ITEMS), rows, preferred_element_type=F32
    ).reshape(C, G, L)

    done(pooled.at[pl.ds(0, NZ - 1)], PO_).wait_recv()
    pool_all = jnp.concatenate([pooled[f] for f in range(NZ)], axis=1)
    pre = pre_self + jnp.dot(pool_all, wf[1024:2048, :], preferred_element_type=F32)
    gate = jax.nn.sigmoid(pre)
    act = pre * gate
    place = 32 * lax.rem(lax.div(lax.broadcasted_iota(jnp.int32, (G, L), 0), Q), 4)
    where_at = lane - place
    acc = jnp.where(where_at == C, jnp.sum(act * act, axis=1, keepdims=True), 0.0)
    for k in range(C):
        acc = jnp.where(where_at == k, jnp.sum(act * cand[k], axis=1, keepdims=True), acc)
    acc = acc.reshape(2, 4, Q, L)
    parts[z] = (acc[:, 0] + acc[:, 1] + acc[:, 2] + acc[:, 3]).reshape(2 * Q, L)
    each(NZ, lambda i: send(parts.at[z], parts.at[z], PC_, on_line(i)[1]))
    done(parts.at[pl.ds(0, NZ - 1)], PC_).wait_recv()
    total = parts[0]
    for f in range(1, NZ):
        total = total + parts[f]
    sums = jnp.concatenate(
        [total[(j // 4) * Q:(j // 4 + 1) * Q, 32 * (j % 4):32 * (j % 4) + 32] for j in range(NZ)],
        axis=0,
    )
    norm = jnp.sqrt(sums[:, C:C + 1] + EPS)
    score = sums / norm
    lane32 = lax.broadcasted_iota(jnp.int32, (G, 32), 1)
    negative = (lane32 >= 1) & (lane32 < C)
    slope = jnp.where(negative, jax.nn.sigmoid(score - score[:, 0:1] + MARGIN), 0.0)
    slope_sum = jnp.sum(slope, axis=1, keepdims=True)
    coef = jnp.where(lane32 == 0, -slope_sum, slope)
    along = jnp.sum(coef * score, axis=1, keepdims=True)
    grad_unit = jnp.zeros((G, L), F32)
    for k in range(C):
        wk = jnp.broadcast_to(coef[:, k:k + 1], (G, L))
        w_b[k] = wk
        grad_unit = grad_unit + wk * cand[k]
    unit = act / norm
    grad_act = (grad_unit - unit * along) / norm
    grad_pre = grad_act * gate * (1.0 + pre * (1.0 - gate))
    gp16 = grad_pre.astype(BF16)
    gpre[z] = gp16
    each(NZ, lambda i: send(gpre.at[z], gpre.at[z], GP_, on_line(i)[1]))

    blank = jnp.zeros((Q, L), F32)
    gp32 = gp16.astype(F32)
    pieces = []
    for j in range(NZ):
        part = gp32[j * Q:(j + 1) * Q]
        pieces.append(jnp.concatenate([part, blank], axis=1))
        pieces.append(jnp.concatenate([blank, part], axis=1))
    gp2 = jnp.concatenate(pieces, axis=0).astype(BF16)
    gw_self = tdot(self2, gp2)
    rw[0:2] = gw_self[:, :L].reshape(2, NY, 2, NX, Q, L)
    rw[2:4] = gw_self[:, L:].reshape(2, NY, 2, NX, Q, L)
    rw[4:8] = tdot(pool_all, gp16).reshape(4, NY, 2, NX, Q, L)
    for k in range(NE):
        hws[k] = rw[:, k // NX, 1 - c, k % NX].reshape(NZ * Q, L).astype(BF16)
    send(hws, hwr, HW_, partner)

    def w2_chunk(h, carry):
        here = lane + h * L
        cols = pl.ds(pl.multiple_of(h * L, L), L)
        acc = jnp.zeros((G, L), F32)
        for k in range(C):
            acc = acc + jnp.where(id_b[K + k] == here, w_b[k], 0.0)
        w2[:, cols] = acc.astype(BF16)
        return carry

    lax.fori_loop(0, ITEMS // L, w2_chunk, 0)
    done(hwr, HW_).wait_recv()
    for k in range(NE):
        own = rw[:, k // NX, c, k % NX].reshape(NZ * Q, L)
        esw[k] = (own + hwr[k].astype(F32)).astype(BF16)
    each(NE, lambda i: send(esw.at[on_face(i)[0]], eww.at[e], EW_, on_face(i)[1]))
    eww[e] = esw[e]

    rt[...] = tdot(w2[...], unit.astype(BF16)).reshape(2, NZ, NY, NX, Q, L)

    done(gpre.at[pl.ds(0, NZ - 1)], GP_).wait_recv()
    gp_all = jnp.concatenate([gpre[f] for f in range(NZ)], axis=1)
    loads[1].wait()
    gps = (ntdot(gp_all, wbp[...]) * inv).astype(BF16)
    rt[...] += tdot(hot[0], gps).reshape(2, NZ, NY, NX, Q, L)
    for k in range(NE):
        hts[k] = rt[1 - c, :, k // NX, k % NX].reshape(NZ * Q, L).astype(BF16)
    send(hts, htr, HT_, partner)
    loads[2].wait()
    gself[...] = ntdot(gp_all, wtop[...])
    o_self[...] = gself[pl.ds(pl.multiple_of(z * Q, Q), Q), :]

    done(htr, HT_).wait_recv()
    for k in range(NE):
        own = rt[c, :, k // NX, k % NX].reshape(NZ * Q, L)
        est[k] = (own + htr[k].astype(F32)).astype(BF16)
    each(NE, lambda i: send(est.at[on_face(i)[0]], ewt.at[e], ET_, on_face(i)[1]))
    ewt[e] = est[e]

    def finish(got, row, summed, final, last):
        done(got.at[pl.ds(0, NE - 1)], row).wait_recv()
        acc = got[0].astype(F32)
        for k in range(1, NE):
            acc = acc + got[k].astype(F32)
        summed[...] = acc.reshape(NZ, Q, L)
        final[z] = summed[z]
        each(NZ, lambda i: send(summed.at[on_line(i)[0]], final.at[z], last, on_line(i)[1]))

    def write(final, last, out):
        done(final.at[pl.ds(0, NZ - 1)], last).wait_recv()
        for f in range(NZ):
            out[:, f * L:(f + 1) * L] = final[f]

    finish(eww, EW_, rsw, oww, OW_)
    finish(ewt, ET_, rst, owt, OT_)
    write(oww, OW_, o_w)
    write(owt, OT_, o_t)

    for ref, row in (
        (qi.at[pl.ds(0, NZ - 1)], QI_), (sf_all.at[pl.ds(0, NZ - 1)], SF_),
        (t_all.at[c, pl.ds(0, NB - 1)], TA_), (t_all.at[c], TP_),
        (pooled.at[pl.ds(0, NZ - 1)], PO_), (parts.at[pl.ds(0, NZ - 1)], PC_),
        (gpre.at[pl.ds(0, NZ - 1)], GP_), (hws, HW_), (hts, HT_),
        (esw.at[pl.ds(0, NE - 1)], EW_), (est.at[pl.ds(0, NE - 1)], ET_),
        (rsw.at[pl.ds(0, NZ - 1)], OW_), (rst.at[pl.ds(0, NZ - 1)], OT_),
    ):
        done(ref, row).wait_send()


def local(table, self_feat, weight, owners, item_rows, importance):
    own = owners[:, :, 0]
    at = (own % 2) * HALF + (own // 2) * 32 + item_rows
    qin = jnp.concatenate(
        [jnp.pad(at, ((0, 0), (0, L - K - C))), jnp.pad(importance, ((0, 0), (0, L - K)))], axis=0
    )
    vmem = pl.BlockSpec(memory_space=pltpu.VMEM)
    out = jax.ShapeDtypeStruct((Q, 1024), F32)
    V = pltpu.VMEM
    return pl.pallas_call(
        kernel,
        out_shape=(out, out, out),
        in_specs=[vmem, vmem, vmem, pl.BlockSpec(memory_space=pl.ANY)],
        out_specs=(vmem, vmem, vmem),
        scratch_shapes=[
            V((2, NB, 32, L), BF16),
            V((NZ, 2 * Q, L), jnp.int32),
            V((NZ, 2 * Q, 512), BF16),
            V((NZ, G, L), BF16),
            V((NZ, 2 * Q, L), F32),
            V((NZ, G, L), BF16),
            V((1 + C, G, ITEMS), BF16),
            V((K + C, G, L), jnp.int32),
            V((K, G, L), F32),
            V((C, G, L), F32),
            V((C, G, L), F32),
            V((G, ITEMS), BF16),
            V((ITEMS, L), BF16),
            V((L, 1024), BF16),
            V((1024, 1024), BF16),
            V((NZ, NY, 2, NX, Q, L), F32),
            V((2, NZ, NY, NX, Q, L), F32),
            V((NE, G, L), BF16),
            V((NE, G, L), BF16),
            V((NE, G, L), BF16),
            V((NE, G, L), BF16),
            V((NE, G, L), BF16),
            V((NE, G, L), BF16),
            V((NE, G, L), BF16),
            V((NE, G, L), BF16),
            V((NZ, Q, L), F32),
            V((NZ, Q, L), F32),
            V((NZ, Q, L), F32),
            V((NZ, Q, L), F32),
            V((G, 1024), F32),
            pltpu.SemaphoreType.DMA((13, 2)),
            pltpu.SemaphoreType.DMA((3,)),
        ],
        compiler_params=pltpu.CompilerParams(
            collective_id=0, has_side_effects=True, vmem_limit_bytes=48 * 1024 * 1024
        ),
    )(table, self_feat, qin, weight)


def solution(mesh):
    both = ("shard", "rep")
    in_specs = (
        P("shard", None), P(both, None), P(), P(both, None, None), P(both, None), P(both, None),
    )
    out_specs = (P(both, None), P(both, None), P(both, None))
    return jax.shard_map(local, mesh=mesh, in_specs=in_specs, out_specs=out_specs, check_vma=False)
```

```python
import jax
import jax.numpy as jnp
from jax import lax
from jax.experimental import pallas as pl
from jax.experimental.pallas import tpu as pltpu
from jax.sharding import PartitionSpec as P

MESH = pl.DeviceIdType.MESH
MARGIN = 0.5
EPS = 1e-06
K = 50
C = 17
NZ, NY, NX = 8, 4, 4
NB = NZ * NY
NE = NY * NX
Q = 8
G = NZ * Q
L = 128
ITEMS = 2048
HALF = ITEMS // 2
F32, BF16 = jnp.float32, jnp.bfloat16
QI_, SF_, TP_, PO_, PC_, GP_, PS_ = range(7)
HALF_, FACE_, LINE_ = 7, 10, 13
TZ_, TY_ = 16, 24


def tdot(a, b):
    return lax.dot_general(a, b, (((0,), (0,)), ((), ())), preferred_element_type=F32)


def ntdot(a, b):
    return lax.dot_general(a, b, (((1,), (1,)), ((), ())), preferred_element_type=F32)


def kernel(
    tab_hbm, sf_hbm, own_hbm, row_hbm, imp_hbm, w_hbm, o_self, o_w, o_t,
    tab, sf, own_in, row_in, imp_in,
    t_all, qi, sf_all, ps_out, ps_in, pooled, parts, gsend, grecv, hot, id_b, cand, w2,
    at_hi, at_lo, cand_hi, cand_lo,
    wf, wtop, wbot, rx, rw, ry, half_out, half_in, face_out, face_in, line_out, line_in,
    sems, wsem,
):
    s = lax.axis_index("shard")
    x = lax.axis_index("rep")
    c = s & 1
    b = s >> 1
    z = b >> 2
    y = b & (NY - 1)
    e = y * NX + x
    partner = (b * 2 + 1 - c, x)

    def on_line(off):
        other = (z + off) & (NZ - 1)
        return other, ((other * NY + y) * 2 + c, x)

    def on_face(off):
        other = (e + off) & (NE - 1)
        return other, ((z * NY + (other >> 2)) * 2 + c, (other & (NX - 1)))

    def send(src, dst, row, to):
        pltpu.make_async_remote_copy(
            src_ref=src, dst_ref=dst, send_sem=sems.at[row, 0], recv_sem=sems.at[row, 1],
            device_id=to, device_id_type=MESH,
        ).start()

    def done(ref, row):
        return pltpu.make_async_remote_copy(
            src_ref=ref, dst_ref=ref, send_sem=sems.at[row, 0], recv_sem=sems.at[row, 1],
            device_id=partner, device_id_type=MESH,
        )

    def each(n, body):
        def step(i, carry):
            body(i)
            return carry
        lax.fori_loop(1, n, step, 0)

    zcol = pl.ds(pl.multiple_of(z * L, L), L)
    loads = [
        pltpu.make_async_copy(w_hbm.at[pl.ds(1024, 1024), zcol], wf, wsem.at[0]),
        pltpu.make_async_copy(w_hbm.at[pl.ds(0, 1024), :], wtop, wsem.at[1]),
        pltpu.make_async_copy(w_hbm.at[pl.ds(1024, 1024), :], wbot, wsem.at[2]),
    ]
    small = [
        pltpu.make_async_copy(src, dst, wsem.at[3 + i])
        for i, (src, dst) in enumerate((
            (own_hbm, own_in), (row_hbm, row_in), (imp_hbm, imp_in), (tab_hbm, tab), (sf_hbm, sf)))
    ]
    for load in small + loads:
        load.start()

    bar = pltpu.get_barrier_semaphore()

    def greet(to):
        pl.semaphore_signal(bar, inc=1, device_id=to, device_id_type=MESH)

    each(NZ, lambda i: greet(on_line(i)[1]))
    each(NE, lambda i: greet(on_face(i)[1]))
    greet(partner)
    for load in small:
        load.wait()
    own = own_in[...]
    at = (own & 1) * HALF + (own >> 1) * 32 + row_in[...]
    qi[z] = jnp.zeros((Q, L), jnp.int32)
    qi[z, :, 0:K + C] = at
    qi[z, :, K + C:2 * K + C] = imp_in[...]
    own_self = sf[...].astype(F32)
    sf_all[z] = jnp.concatenate([own_self[:, :512], own_self[:, 512:]], axis=0).astype(BF16)
    t_all[c, b] = tab[:, zcol]
    pl.semaphore_wait(bar, NZ - 1 + NE - 1 + 1)

    each(NZ, lambda i: send(qi.at[z], qi.at[z], QI_, on_line(i)[1]))

    for k in (4, 3, 5, 2, 6, 1, 7):
        to_z = (z - k) & (NZ - 1)
        cols = pl.ds(pl.multiple_of(to_z * L, L), L)
        send(tab.at[:, cols], t_all.at[c, b], TZ_ + k, ((to_z * NY + y) * 2 + c, x))

    def pass_on(k):
        at = t_all.at[c, ((z + k) & (NZ - 1)) * NY + y]
        for dy in range(1, NY):
            send(at, at, TY_ + k, ((z * NY + ((y + dy) & (NY - 1))) * 2 + c, x))
        send(at, at, TP_, partner)

    pass_on(0)
    loads[1].wait()
    own_pre = jnp.dot(sf[...], wtop[...], preferred_element_type=F32)
    for f in range(NZ):
        ps_out[f] = own_pre[:, f * L:(f + 1) * L]
    each(NZ, lambda i: send(ps_out.at[on_line(i)[0]], ps_in.at[z], PS_, on_line(i)[1]))
    ps_in[z] = ps_out[z]
    for k in (1, 7, 2, 6, 3, 5, 4):
        done(t_all.at[c, b], TZ_ + k).wait_recv()
        pass_on(k)

    done(qi.at[pl.ds(0, NZ - 1)], QI_).wait_recv()
    ids = qi[...].reshape(G, L)
    imp = ids.astype(F32)
    lane = lax.broadcasted_iota(jnp.int32, (G, L), 1)
    query = lax.broadcasted_iota(jnp.int32, (G, L), 0) & (Q - 1)
    weighed = (lane >= K + C) & (lane < 2 * K + C)
    inv = 1.0 / jnp.sum(jnp.where(weighed, imp, 0.0), axis=1, keepdims=True)
    ids_hi = (ids >> 7) * Q + query
    ids_lo = ids & (L - 1)

    def spread(values, k):
        return jnp.broadcast_to(values[:, k:k + 1], (G, L))

    def pair(one, two):
        both = jnp.concatenate([one.reshape(NZ, Q, L), two.reshape(NZ, Q, L)], axis=1)
        return both.astype(BF16)

    def hit(values, k, weight=1.0):
        return jnp.where(spread(values, k) == lane, weight, 0.0)

    def outer(out, hi, lo):
        for m in range(NZ // 2):
            one = tdot(hi[2 * m], lo[2 * m])
            two = tdot(hi[2 * m + 1], lo[2 * m + 1])
            for h in range(ITEMS // L):
                both = jnp.concatenate([one[h * Q:(h + 1) * Q], two[h * Q:(h + 1) * Q]], axis=0)
                out[2 * m * Q:2 * (m + 1) * Q, h * L:(h + 1) * L] = both.astype(BF16)

    for m in range(K // 2):
        k = 2 * m
        at_hi[:, k * Q:(k + 2) * Q] = pair(hit(ids_hi, k), hit(ids_hi, k + 1))
        at_lo[:, k * Q:(k + 2) * Q] = pair(
            hit(ids_lo, k, spread(imp, K + C + k)), hit(ids_lo, k + 1, spread(imp, K + C + k + 1)))
    outer(hot.at[0], at_hi, at_lo)

    for k in (0, 1, 7, 2, 6, 3, 5, 4):
        first = ((z + k) & (NZ - 1)) * NY
        done(t_all.at[c, pl.ds(first, NY - 1)], TY_ + k).wait_recv()
        for dy in range(1, NY):
            at = t_all.at[c, first + ((y + dy) & (NY - 1))]
            send(at, at, TP_, partner)
    done(t_all.at[1 - c], TP_).wait_recv()

    rows = t_all[...].reshape(ITEMS, L)
    mine = jnp.dot(hot[0], rows, preferred_element_type=F32) * inv
    pooled[z] = mine.astype(BF16)
    each(NZ, lambda i: send(pooled.at[z], pooled.at[z], PO_, on_line(i)[1]))
    for k in range(C):
        id_b[k] = spread(ids, K + k)

    def hot_chunk(h, carry):
        here = lane + h * L
        cols = pl.ds(pl.multiple_of(h * L, L), L)
        for k in range(C):
            hot[1 + k, :, cols] = jnp.where(id_b[k] == here, 1.0, 0.0).astype(BF16)
        return carry

    lax.fori_loop(0, ITEMS // L, hot_chunk, 0)
    cand[...] = jnp.dot(
        hot[1:1 + C].reshape(C * G, ITEMS), rows, preferred_element_type=F32
    ).reshape(C, G, L)

    zero = jnp.zeros((G, L), F32)
    for m in range((C + 1) // 2):
        k = K + 2 * m
        last = zero if 2 * m + 1 == C else hit(ids_hi, k + 1)
        cand_hi[:, 2 * m * Q:(2 * m + 2) * Q] = pair(hit(ids_hi, k), last)
    loads[0].wait()
    done(pooled.at[pl.ds(0, NZ - 1)], PO_).wait_recv()
    pool_all = jnp.concatenate([pooled[f] for f in range(NZ)], axis=1)
    done(ps_in.at[pl.ds(0, NZ - 1)], PS_).wait_recv()
    pre = ps_in[...].reshape(G, L) + jnp.dot(pool_all, wf[...], preferred_element_type=F32)
    gate = jax.nn.sigmoid(pre)
    act = pre * gate
    place = 32 * lax.rem(lax.div(lax.broadcasted_iota(jnp.int32, (G, L), 0), Q), 4)
    where_at = lane - place
    acc = jnp.where(where_at == C, jnp.sum(act * act, axis=1, keepdims=True), 0.0)
    for k in range(C):
        acc = jnp.where(where_at == k, jnp.sum(act * cand[k], axis=1, keepdims=True), acc)
    acc = acc.reshape(2, 4, Q, L)
    parts[z] = (acc[:, 0] + acc[:, 1] + acc[:, 2] + acc[:, 3]).reshape(2 * Q, L)
    each(NZ, lambda i: send(parts.at[z], parts.at[z], PC_, on_line(i)[1]))
    each(NZ, lambda i: send(sf_all.at[z], sf_all.at[z], SF_, on_line(i)[1]))
    done(parts.at[pl.ds(0, NZ - 1)], PC_).wait_recv()
    total = parts[0]
    for f in range(1, NZ):
        total = total + parts[f]
    sums = jnp.concatenate(
        [total[(j // 4) * Q:(j // 4 + 1) * Q, 32 * (j % 4):32 * (j % 4) + 32] for j in range(NZ)],
        axis=0,
    )
    norm = jnp.sqrt(sums[:, C:C + 1] + EPS)
    score = sums / norm
    lane32 = lax.broadcasted_iota(jnp.int32, (G, 32), 1)
    negative = (lane32 >= 1) & (lane32 < C)
    slope = jnp.where(negative, jax.nn.sigmoid(score - score[:, 0:1] + MARGIN), 0.0)
    slope_sum = jnp.sum(slope, axis=1, keepdims=True)
    coef = jnp.where(lane32 == 0, -slope_sum, slope)
    along = jnp.sum(coef * score, axis=1, keepdims=True)
    grad_unit = jnp.zeros((G, L), F32)
    for k in range(C):
        grad_unit = grad_unit + spread(coef, k) * cand[k]
    unit = act / norm
    grad_act = (grad_unit - unit * along) / norm
    grad_pre = grad_act * gate * (1.0 + pre * (1.0 - gate))
    gp16 = grad_pre.astype(BF16)
    gp32 = gp16.astype(F32)

    def swap(n, half_of):
        for k in range(NE):
            half_out[n, k] = half_of(1 - c, k // NX, k % NX).reshape(NZ * Q, L).astype(BF16)
        send(half_out.at[n], half_in.at[n], HALF_ + n, partner)

    def scatter(n, half_of):
        done(half_in.at[n], HALF_ + n).wait_recv()
        for k in range(NE):
            own = half_of(c, k // NX, k % NX).reshape(NZ * Q, L)
            face_out[n, k] = (own + half_in[n, k].astype(F32)).astype(BF16)
        each(NE, lambda i: send(
            face_out.at[n, on_face(i)[0]], face_in.at[n, e], FACE_ + n, on_face(i)[1]))
        face_in[n, e] = face_out[n, e]

    def half_x(core, yy, xx):
        return rx[core, :, yy, xx]

    def half_w(core, yy, xx):
        return rw[:, yy, core, xx]

    def half_y(core, yy, xx):
        return ry[core, :, yy, xx]

    rx[...] = tdot(hot[0], (gp32 * inv).astype(BF16)).reshape(2, NZ, NY, NX, Q, L)
    swap(0, half_x)

    for m in range((C + 1) // 2):
        k = 2 * m
        last = zero if k + 1 == C else hit(ids_lo, K + k + 1, spread(coef, k + 1))
        cand_lo[:, k * Q:(k + 2) * Q] = pair(hit(ids_lo, K + k, spread(coef, k)), last)
    outer(w2, cand_hi, cand_lo)
    ry[...] = tdot(w2[...], unit.astype(BF16)).reshape(2, NZ, NY, NX, Q, L)
    swap(1, half_y)
    scatter(0, half_x)

    done(sf_all.at[pl.ds(0, NZ - 1)], SF_).wait_recv()
    self2 = sf_all[...].reshape(2 * G, 512)
    blank = jnp.zeros((Q, L), F32)
    pieces = []
    for j in range(NZ):
        part = gp32[j * Q:(j + 1) * Q]
        pieces.append(jnp.concatenate([part, blank], axis=1))
        pieces.append(jnp.concatenate([blank, part], axis=1))
    gp2 = jnp.concatenate(pieces, axis=0).astype(BF16)
    gw_self = tdot(self2, gp2)
    rw[0:2] = gw_self[:, :L].reshape(2, NY, 2, NX, Q, L)
    rw[2:4] = gw_self[:, L:].reshape(2, NY, 2, NX, Q, L)
    rw[4:8] = tdot(pool_all, gp16).reshape(4, NY, 2, NX, Q, L)
    swap(2, half_w)
    scatter(1, half_y)

    gsend[...] = gp32.reshape(NZ, Q, L)
    each(NZ, lambda i: send(gsend.at[on_line(i)[0]], grecv.at[z], GP_, on_line(i)[1]))
    grecv[z] = gsend[z]
    scatter(2, half_w)

    done(grecv.at[pl.ds(0, NZ - 1)], GP_).wait_recv()
    gp_own = jnp.concatenate([grecv[f] for f in range(NZ)], axis=1).astype(BF16)
    o_self[...] = ntdot(gp_own, wtop[...])

    def finish(n):
        done(face_in.at[n, pl.ds(0, NE - 1)], FACE_ + n).wait_recv()
        acc = face_in[n, 0].astype(F32)
        for k in range(1, NE):
            acc = acc + face_in[n, k].astype(F32)
        line_out[n] = acc.reshape(NZ, Q, L)
        line_in[n, z] = line_out[n, z]
        each(NZ, lambda i: send(
            line_out.at[n, on_line(i)[0]], line_in.at[n, z], LINE_ + n, on_line(i)[1]))

    def row_sums(n):
        done(line_in.at[n, pl.ds(0, NZ - 1)], LINE_ + n).wait_recv()
        return jnp.concatenate([line_in[n, f] for f in range(NZ)], axis=1)

    finish(0)
    finish(1)
    finish(2)
    before = row_sums(0)
    rest = before - before.astype(BF16).astype(F32)
    loads[2].wait()
    after = ntdot(jnp.concatenate([before, rest], axis=0).astype(BF16), wbot[...])
    o_t[...] = after[0:Q] + after[Q:2 * Q] + row_sums(1)
    o_w[...] = row_sums(2)

    for ref, row in (
        (qi.at[pl.ds(0, NZ - 1)], QI_), (sf_all.at[pl.ds(0, NZ - 1)], SF_),
        (t_all.at[c], TP_), (pooled.at[pl.ds(0, NZ - 1)], PO_),
        (parts.at[pl.ds(0, NZ - 1)], PC_), (gsend.at[pl.ds(0, NZ - 1)], GP_),
        (ps_out.at[pl.ds(0, NZ - 1)], PS_),
    ):
        done(ref, row).wait_send()
    for k in range(NZ):
        if k:
            done(t_all.at[c, b], TZ_ + k).wait_send()
        done(t_all.at[c, pl.ds(0, NY - 1)], TY_ + k).wait_send()
    for n in range(3):
        done(half_out.at[n], HALF_ + n).wait_send()
        done(face_out.at[n, pl.ds(0, NE - 1)], FACE_ + n).wait_send()
        done(line_out.at[n, pl.ds(0, NZ - 1)], LINE_ + n).wait_send()


def hand_over(a, b, c, to_a, to_b, to_c):
    to_a[...] = a[...]
    to_b[...] = b[...]
    to_c[...] = c[...]


def local(table, self_feat, weight, owners, item_rows, importance):
    vmem = pl.BlockSpec(memory_space=pltpu.VMEM)
    hbm = pl.BlockSpec(memory_space=pl.ANY)
    out = jax.ShapeDtypeStruct((Q, 1024), F32)
    V = pltpu.VMEM
    grads = pl.pallas_call(
        kernel,
        out_shape=(out, out, out),
        in_specs=[hbm] * 6,
        out_specs=(vmem, vmem, vmem),
        scratch_shapes=[
            V((32, 1024), BF16),
            V((Q, 1024), BF16),
            V((Q, K + C), jnp.int32),
            V((Q, K + C), jnp.int32),
            V((Q, K), jnp.int32),
            V((2, NB, 32, L), BF16),
            V((NZ, Q, L), jnp.int32),
            V((NZ, 2 * Q, 512), BF16),
            V((NZ, Q, L), F32),
            V((NZ, Q, L), F32),
            V((NZ, G, L), BF16),
            V((NZ, 2 * Q, L), F32),
            V((NZ, Q, L), F32),
            V((NZ, Q, L), F32),
            V((1 + C, G, ITEMS), BF16),
            V((C, G, L), jnp.int32),
            V((C, G, L), F32),
            V((G, ITEMS), BF16),
            V((NZ, K * Q, L), BF16),
            V((NZ, K * Q, L), BF16),
            V((NZ, (C + 1) * Q, L), BF16),
            V((NZ, (C + 1) * Q, L), BF16),
            V((1024, L), BF16),
            V((1024, 1024), BF16),
            V((1024, 1024), BF16),
            V((2, NZ, NY, NX, Q, L), F32),
            V((NZ, NY, 2, NX, Q, L), F32),
            V((2, NZ, NY, NX, Q, L), F32),
            V((3, NE, G, L), BF16),
            V((3, NE, G, L), BF16),
            V((3, NE, G, L), BF16),
            V((3, NE, G, L), BF16),
            V((3, NZ, Q, L), F32),
            V((3, NZ, Q, L), F32),
            pltpu.SemaphoreType.DMA((32, 2)),
            pltpu.SemaphoreType.DMA((8,)),
        ],
        compiler_params=pltpu.CompilerParams(
            collective_id=0, has_side_effects=True, vmem_limit_bytes=62 * 1024 * 1024
        ),
    )(table, self_feat, owners.reshape(Q, K + C), item_rows, importance, weight)
    return pl.pallas_call(
        hand_over, out_shape=(out, out, out), in_specs=[vmem] * 3, out_specs=(vmem,) * 3
    )(*grads)


def solution(mesh):
    both = ("shard", "rep")
    in_specs = (
        P("shard", None), P(both, None), P(), P(both, None, None), P(both, None), P(both, None),
    )
    out_specs = (P(both, None), P(both, None), P(both, None))
    return jax.shard_map(local, mesh=mesh, in_specs=in_specs, out_specs=out_specs, check_vma=False)
```

```python
import jax
import jax.numpy as jnp
from jax import lax
from jax.experimental import pallas as pl
from jax.experimental.pallas import tpu as pltpu
from jax.sharding import PartitionSpec as P

MESH = pl.DeviceIdType.MESH
MARGIN = 0.5
EPS = 1e-06
K = 50
C = 17
NZ, NY, NX = 8, 4, 4
NB = NZ * NY
NE = NY * NX
Q = 8
G = NZ * Q
L = 128
ITEMS = 2048
HALF = ITEMS // 2
F32, BF16 = jnp.float32, jnp.bfloat16
QI_, SF_, TP_, PO_, PC_, GP_, PS_, HP_, GX_ = range(9)
HALF_, FACE_, LINE_ = 9, 12, 15
TZ_, TY_ = 18, 26


def tdot(a, b):
    return lax.dot_general(a, b, (((0,), (0,)), ((), ())), preferred_element_type=F32)


def ntdot(a, b):
    return lax.dot_general(a, b, (((1,), (1,)), ((), ())), preferred_element_type=F32)


def kernel(
    tab_hbm, sf_hbm, own_hbm, row_hbm, imp_hbm, w_hbm, o_self, o_w, o_t,
    tab, sf, own_in, row_in, imp_in,
    t_all, qi, sf_all, ps_out, ps_in, pooled, parts, gsend, grecv, hot, id_b, cand, w2, hot_in, gx_out, gx_in,
    at_hi, at_lo, cand_hi, cand_lo,
    wf, wtop, wbot, rx, rw, ry, half_out, half_in, face_out, face_in, line_out, line_in,
    sems, wsem,
):
    s = lax.axis_index("shard")
    x = lax.axis_index("rep")
    c = s & 1
    b = s >> 1
    z = b >> 2
    y = b & (NY - 1)
    e = y * NX + x
    partner = (b * 2 + 1 - c, x)

    def on_line(off):
        other = (z + off) & (NZ - 1)
        return other, ((other * NY + y) * 2 + c, x)

    def on_face(off):
        other = (e + off) & (NE - 1)
        return other, ((z * NY + (other >> 2)) * 2 + c, (other & (NX - 1)))

    def send(src, dst, row, to):
        pltpu.make_async_remote_copy(
            src_ref=src, dst_ref=dst, send_sem=sems.at[row, 0], recv_sem=sems.at[row, 1],
            device_id=to, device_id_type=MESH,
        ).start()

    def done(ref, row):
        return pltpu.make_async_remote_copy(
            src_ref=ref, dst_ref=ref, send_sem=sems.at[row, 0], recv_sem=sems.at[row, 1],
            device_id=partner, device_id_type=MESH,
        )

    def each(n, body):
        def step(i, carry):
            body(i)
            return carry
        lax.fori_loop(1, n, step, 0)

    zcol = pl.ds(pl.multiple_of(z * L, L), L)
    loads = [
        pltpu.make_async_copy(w_hbm.at[pl.ds(1024, 1024), zcol], wf, wsem.at[0]),
        pltpu.make_async_copy(w_hbm.at[pl.ds(0, 1024), :], wtop, wsem.at[1]),
        pltpu.make_async_copy(w_hbm.at[pl.ds(1024, 1024), :], wbot, wsem.at[2]),
    ]
    small = [
        pltpu.make_async_copy(src, dst, wsem.at[3 + i])
        for i, (src, dst) in enumerate((
            (own_hbm, own_in), (row_hbm, row_in), (imp_hbm, imp_in), (tab_hbm, tab), (sf_hbm, sf)))
    ]
    for load in small + loads:
        load.start()

    bar = pltpu.get_barrier_semaphore()

    def greet(to):
        pl.semaphore_signal(bar, inc=1, device_id=to, device_id_type=MESH)

    each(NZ, lambda i: greet(on_line(i)[1]))
    each(NE, lambda i: greet(on_face(i)[1]))
    greet(partner)
    small[3].wait()
    t_all[c, b] = tab[:, zcol]
    pl.semaphore_wait(bar, NZ - 1 + NE - 1 + 1)

    for k in (4, 3, 5, 2, 6, 1, 7):
        to_z = (z - k) & (NZ - 1)
        cols = pl.ds(pl.multiple_of(to_z * L, L), L)
        send(tab.at[:, cols], t_all.at[c, b], TZ_ + k, ((to_z * NY + y) * 2 + c, x))

    def pass_on(k):
        at = t_all.at[c, ((z + k) & (NZ - 1)) * NY + y]
        for dy in range(1, NY):
            send(at, at, TY_ + k, ((z * NY + ((y + dy) & (NY - 1))) * 2 + c, x))
        send(at, at, TP_, partner)

    pass_on(0)
    for load in small[:3]:
        load.wait()
    own = own_in[...]
    at = (own & 1) * HALF + (own >> 1) * 32 + row_in[...]
    qi[z] = jnp.zeros((Q, L), jnp.int32)
    qi[z, :, 0:K + C] = at
    qi[z, :, K + C:2 * K + C] = imp_in[...]
    each(NZ, lambda i: send(qi.at[z], qi.at[z], QI_, on_line(i)[1]))
    for k in (1, 7, 2, 6, 3, 5, 4):
        done(t_all.at[c, b], TZ_ + k).wait_recv()
        pass_on(k)

    small[4].wait()
    loads[1].wait()
    own_pre = jnp.dot(sf[...], wtop[...], preferred_element_type=F32)
    for f in range(NZ):
        ps_out[f] = own_pre[:, f * L:(f + 1) * L]
    each(NZ, lambda i: send(ps_out.at[on_line(i)[0]], ps_in.at[z], PS_, on_line(i)[1]))
    ps_in[z] = ps_out[z]
    own_self = sf[...].astype(F32)
    sf_all[z] = jnp.concatenate([own_self[:, :512], own_self[:, 512:]], axis=0).astype(BF16)
    each(NZ, lambda i: send(sf_all.at[z], sf_all.at[z], SF_, on_line(i)[1]))

    done(qi.at[pl.ds(0, NZ - 1)], QI_).wait_recv()
    ids = qi[...].reshape(G, L)
    imp = ids.astype(F32)
    lane = lax.broadcasted_iota(jnp.int32, (G, L), 1)
    query = lax.broadcasted_iota(jnp.int32, (G, L), 0) & (Q - 1)
    weighed = (lane >= K + C) & (lane < 2 * K + C)
    inv = 1.0 / jnp.sum(jnp.where(weighed, imp, 0.0), axis=1, keepdims=True)
    ids_hi = (ids >> 7) * Q + query
    ids_lo = ids & (L - 1)

    def spread(values, k):
        return jnp.broadcast_to(values[:, k:k + 1], (G, L))

    def pair(one, two):
        both = jnp.concatenate([one.reshape(NZ, Q, L), two.reshape(NZ, Q, L)], axis=1)
        return both.astype(BF16)

    def hit(values, k, weight=1.0):
        return jnp.where(spread(values, k) == lane, weight, 0.0)

    def outer(out, hi, lo):
        for m in range(NZ // 2):
            one = tdot(hi[2 * m], lo[2 * m])
            two = tdot(hi[2 * m + 1], lo[2 * m + 1])
            for h in range(ITEMS // L):
                both = jnp.concatenate([one[h * Q:(h + 1) * Q], two[h * Q:(h + 1) * Q]], axis=0)
                out[2 * m * Q:2 * (m + 1) * Q, h * L:(h + 1) * L] = both.astype(BF16)

    for m in range(K // 2):
        k = 2 * m
        at_hi[:, k * Q:(k + 2) * Q] = pair(hit(ids_hi, k), hit(ids_hi, k + 1))
        at_lo[:, k * Q:(k + 2) * Q] = pair(
            hit(ids_lo, k, spread(imp, K + C + k)), hit(ids_lo, k + 1, spread(imp, K + C + k + 1)))
    outer(hot.at[0], at_hi, at_lo)

    for k in (0, 1, 7, 2, 6, 3, 5, 4):
        first = ((z + k) & (NZ - 1)) * NY
        done(t_all.at[c, pl.ds(first, NY - 1)], TY_ + k).wait_recv()
        for dy in range(1, NY):
            at = t_all.at[c, first + ((y + dy) & (NY - 1))]
            send(at, at, TP_, partner)
    done(t_all.at[1 - c], TP_).wait_recv()

    rows = t_all[...].reshape(ITEMS, L)
    mine = jnp.dot(hot[0], rows, preferred_element_type=F32) * inv
    pooled[z] = mine.astype(BF16)
    each(NZ, lambda i: send(pooled.at[z], pooled.at[z], PO_, on_line(i)[1]))
    half = pl.ds(pl.multiple_of(c * HALF, HALF), HALF)
    other = pl.ds(pl.multiple_of((1 - c) * HALF, HALF), HALF)
    send(hot.at[0, :, other], hot_in, HP_, partner)
    for k in range(C):
        id_b[k] = spread(ids, K + k)

    def hot_chunk(h, carry):
        here = lane + h * L
        cols = pl.ds(pl.multiple_of(h * L, L), L)
        for k in range(C):
            hot[1 + k, :, cols] = jnp.where(id_b[k] == here, 1.0, 0.0).astype(BF16)
        return carry

    lax.fori_loop(0, ITEMS // L, hot_chunk, 0)
    cand[...] = jnp.dot(
        hot[1:1 + C].reshape(C * G, ITEMS), rows, preferred_element_type=F32
    ).reshape(C, G, L)

    zero = jnp.zeros((G, L), F32)
    for m in range((C + 1) // 2):
        k = K + 2 * m
        last = zero if 2 * m + 1 == C else hit(ids_hi, k + 1)
        cand_hi[:, 2 * m * Q:(2 * m + 2) * Q] = pair(hit(ids_hi, k), last)
    loads[0].wait()
    done(pooled.at[pl.ds(0, NZ - 1)], PO_).wait_recv()
    pool_all = jnp.concatenate([pooled[f] for f in range(NZ)], axis=1)
    done(ps_in.at[pl.ds(0, NZ - 1)], PS_).wait_recv()
    pre = ps_in[...].reshape(G, L) + jnp.dot(pool_all, wf[...], preferred_element_type=F32)
    gate = jax.nn.sigmoid(pre)
    act = pre * gate
    place = 32 * lax.rem(lax.div(lax.broadcasted_iota(jnp.int32, (G, L), 0), Q), 4)
    where_at = lane - place
    acc = jnp.where(where_at == C, jnp.sum(act * act, axis=1, keepdims=True), 0.0)
    for k in range(C):
        acc = jnp.where(where_at == k, jnp.sum(act * cand[k], axis=1, keepdims=True), acc)
    acc = acc.reshape(2, 4, Q, L)
    parts[z] = (acc[:, 0] + acc[:, 1] + acc[:, 2] + acc[:, 3]).reshape(2 * Q, L)
    each(NZ, lambda i: send(parts.at[z], parts.at[z], PC_, on_line(i)[1]))
    done(parts.at[pl.ds(0, NZ - 1)], PC_).wait_recv()
    total = parts[0]
    for f in range(1, NZ):
        total = total + parts[f]
    sums = jnp.concatenate(
        [total[(j // 4) * Q:(j // 4 + 1) * Q, 32 * (j % 4):32 * (j % 4) + 32] for j in range(NZ)],
        axis=0,
    )
    norm = jnp.sqrt(sums[:, C:C + 1] + EPS)
    score = sums / norm
    lane32 = lax.broadcasted_iota(jnp.int32, (G, 32), 1)
    negative = (lane32 >= 1) & (lane32 < C)
    slope = jnp.where(negative, jax.nn.sigmoid(score - score[:, 0:1] + MARGIN), 0.0)
    slope_sum = jnp.sum(slope, axis=1, keepdims=True)
    coef = jnp.where(lane32 == 0, -slope_sum, slope)
    along = jnp.sum(coef * score, axis=1, keepdims=True)
    grad_unit = jnp.zeros((G, L), F32)
    for k in range(C):
        grad_unit = grad_unit + spread(coef, k) * cand[k]
    unit = act / norm
    grad_act = (grad_unit - unit * along) / norm
    grad_pre = grad_act * gate * (1.0 + pre * (1.0 - gate))
    gp16 = grad_pre.astype(BF16)
    gp32 = gp16.astype(F32)

    def swap(n, half_of):
        for k in range(NE):
            half_out[n, k] = half_of(1 - c, k // NX, k % NX).reshape(NZ * Q, L).astype(BF16)
        send(half_out.at[n], half_in.at[n], HALF_ + n, partner)

    def scatter(n, half_of):
        done(half_in.at[n], HALF_ + n).wait_recv()
        for k in range(NE):
            own = half_of(c, k // NX, k % NX).reshape(NZ * Q, L)
            face_out[n, k] = (own + half_in[n, k].astype(F32)).astype(BF16)
        spread_out(n)

    def spread_out(n):
        each(NE, lambda i: send(
            face_out.at[n, on_face(i)[0]], face_in.at[n, e], FACE_ + n, on_face(i)[1]))
        face_in[n, e] = face_out[n, e]

    def half_w(core, yy, xx):
        return rw[:, yy, core, xx]

    def half_y(core, yy, xx):
        return ry[core, :, yy, xx]

    gx_out[...] = (gp32 * inv).astype(BF16)
    send(gx_out, gx_in, GX_, partner)

    for m in range((C + 1) // 2):
        k = 2 * m
        last = zero if k + 1 == C else hit(ids_lo, K + k + 1, spread(coef, k + 1))
        cand_lo[:, k * Q:(k + 2) * Q] = pair(hit(ids_lo, K + k, spread(coef, k)), last)
    outer(w2, cand_hi, cand_lo)
    ry[...] = tdot(w2[...], unit.astype(BF16)).reshape(2, NZ, NY, NX, Q, L)
    swap(1, half_y)
    done(hot_in, HP_).wait_recv()
    mine_x = tdot(hot[0, :, half], gx_out[...])
    done(gx_in, GX_).wait_recv()
    rx[...] = (mine_x + tdot(hot_in[...], gx_in[...])).reshape(NZ, NY, NX, Q, L)
    for k in range(NE):
        face_out[0, k] = rx[:, k // NX, k % NX].reshape(NZ * Q, L).astype(BF16)
    spread_out(0)

    done(sf_all.at[pl.ds(0, NZ - 1)], SF_).wait_recv()
    self2 = sf_all[...].reshape(2 * G, 512)
    blank = jnp.zeros((Q, L), F32)
    pieces = []
    for j in range(NZ):
        part = gp32[j * Q:(j + 1) * Q]
        pieces.append(jnp.concatenate([part, blank], axis=1))
        pieces.append(jnp.concatenate([blank, part], axis=1))
    gp2 = jnp.concatenate(pieces, axis=0).astype(BF16)
    gw_self = tdot(self2, gp2)
    rw[0:2] = gw_self[:, :L].reshape(2, NY, 2, NX, Q, L)
    rw[2:4] = gw_self[:, L:].reshape(2, NY, 2, NX, Q, L)
    rw[4:8] = tdot(pool_all, gp16).reshape(4, NY, 2, NX, Q, L)
    swap(2, half_w)
    scatter(1, half_y)

    gsend[...] = gp32.reshape(NZ, Q, L)
    each(NZ, lambda i: send(gsend.at[on_line(i)[0]], grecv.at[z], GP_, on_line(i)[1]))
    grecv[z] = gsend[z]
    scatter(2, half_w)

    done(grecv.at[pl.ds(0, NZ - 1)], GP_).wait_recv()
    gp_own = jnp.concatenate([grecv[f] for f in range(NZ)], axis=1).astype(BF16)
    o_self[...] = ntdot(gp_own, wtop[...])

    def finish(n):
        done(face_in.at[n, pl.ds(0, NE - 1)], FACE_ + n).wait_recv()
        acc = face_in[n, 0].astype(F32)
        for k in range(1, NE):
            acc = acc + face_in[n, k].astype(F32)
        line_out[n] = acc.reshape(NZ, Q, L)
        line_in[n, z] = line_out[n, z]
        each(NZ, lambda i: send(
            line_out.at[n, on_line(i)[0]], line_in.at[n, z], LINE_ + n, on_line(i)[1]))

    def row_sums(n):
        done(line_in.at[n, pl.ds(0, NZ - 1)], LINE_ + n).wait_recv()
        return jnp.concatenate([line_in[n, f] for f in range(NZ)], axis=1)

    finish(0)
    finish(1)
    finish(2)
    before = row_sums(0)
    rest = before - before.astype(BF16).astype(F32)
    loads[2].wait()
    after = ntdot(jnp.concatenate([before, rest], axis=0).astype(BF16), wbot[...])
    o_t[...] = after[0:Q] + after[Q:2 * Q] + row_sums(1)
    o_w[...] = row_sums(2)

    for ref, row in (
        (qi.at[pl.ds(0, NZ - 1)], QI_), (sf_all.at[pl.ds(0, NZ - 1)], SF_),
        (t_all.at[c], TP_), (pooled.at[pl.ds(0, NZ - 1)], PO_),
        (parts.at[pl.ds(0, NZ - 1)], PC_), (gsend.at[pl.ds(0, NZ - 1)], GP_),
        (ps_out.at[pl.ds(0, NZ - 1)], PS_), (hot.at[0, :, other], HP_), (gx_out, GX_),
    ):
        done(ref, row).wait_send()
    for k in range(NZ):
        if k:
            done(t_all.at[c, b], TZ_ + k).wait_send()
        done(t_all.at[c, pl.ds(0, NY - 1)], TY_ + k).wait_send()
    for n in range(3):
        if n:
            done(half_out.at[n], HALF_ + n).wait_send()
        done(face_out.at[n, pl.ds(0, NE - 1)], FACE_ + n).wait_send()
        done(line_out.at[n, pl.ds(0, NZ - 1)], LINE_ + n).wait_send()


def hand_over(a, b, c, to_a, to_b, to_c):
    to_a[...] = a[...]
    to_b[...] = b[...]
    to_c[...] = c[...]


def local(table, self_feat, weight, owners, item_rows, importance):
    vmem = pl.BlockSpec(memory_space=pltpu.VMEM)
    hbm = pl.BlockSpec(memory_space=pl.ANY)
    out = jax.ShapeDtypeStruct((Q, 1024), F32)
    V = pltpu.VMEM
    grads = pl.pallas_call(
        kernel,
        out_shape=(out, out, out),
        in_specs=[hbm] * 6,
        out_specs=(vmem, vmem, vmem),
        scratch_shapes=[
            V((32, 1024), BF16),
            V((Q, 1024), BF16),
            V((Q, K + C), jnp.int32),
            V((Q, K + C), jnp.int32),
            V((Q, K), jnp.int32),
            V((2, NB, 32, L), BF16),
            V((NZ, Q, L), jnp.int32),
            V((NZ, 2 * Q, 512), BF16),
            V((NZ, Q, L), F32),
            V((NZ, Q, L), F32),
            V((NZ, G, L), BF16),
            V((NZ, 2 * Q, L), F32),
            V((NZ, Q, L), F32),
            V((NZ, Q, L), F32),
            V((1 + C, G, ITEMS), BF16),
            V((C, G, L), jnp.int32),
            V((C, G, L), F32),
            V((G, ITEMS), BF16),
            V((G, HALF), BF16),
            V((G, L), BF16),
            V((G, L), BF16),
            V((NZ, K * Q, L), BF16),
            V((NZ, K * Q, L), BF16),
            V((NZ, (C + 1) * Q, L), BF16),
            V((NZ, (C + 1) * Q, L), BF16),
            V((1024, L), BF16),
            V((1024, 1024), BF16),
            V((1024, 1024), BF16),
            V((NZ, NY, NX, Q, L), F32),
            V((NZ, NY, 2, NX, Q, L), F32),
            V((2, NZ, NY, NX, Q, L), F32),
            V((3, NE, G, L), BF16),
            V((3, NE, G, L), BF16),
            V((3, NE, G, L), BF16),
            V((3, NE, G, L), BF16),
            V((3, NZ, Q, L), F32),
            V((3, NZ, Q, L), F32),
            pltpu.SemaphoreType.DMA((34, 2)),
            pltpu.SemaphoreType.DMA((8,)),
        ],
        compiler_params=pltpu.CompilerParams(
            collective_id=0, has_side_effects=True, vmem_limit_bytes=62 * 1024 * 1024
        ),
    )(table, self_feat, owners.reshape(Q, K + C), item_rows, importance, weight)
    return pl.pallas_call(
        hand_over, out_shape=(out, out, out), in_specs=[vmem] * 3, out_specs=(vmem,) * 3
    )(*grads)


def solution(mesh):
    both = ("shard", "rep")
    in_specs = (
        P("shard", None), P(both, None), P(), P(both, None, None), P(both, None), P(both, None),
    )
    out_specs = (P(both, None), P(both, None), P(both, None))
    return jax.shard_map(local, mesh=mesh, in_specs=in_specs, out_specs=out_specs, check_vma=False)
```

```python
import jax
import jax.numpy as jnp
from jax import lax
from jax.experimental import pallas as pl
from jax.experimental.pallas import tpu as pltpu
from jax.sharding import PartitionSpec as P

MESH = pl.DeviceIdType.MESH
MARGIN = 0.5
EPS = 1e-06
K = 50
C = 17
NZ, NY, NX = 8, 4, 4
NB = NZ * NY
NE = NY * NX
Q = 8
G = NZ * Q
L = 128
ITEMS = 2048
HALF = ITEMS // 2
F32, BF16 = jnp.float32, jnp.bfloat16
QI_, SF_, TP_, PO_, PC_, GP_, PS_, HP_, GX_ = range(9)
HALF_, LINE_, FACE_ = 9, 12, 15
TZ_, TY_ = 21, 29


def tdot(a, b):
    return lax.dot_general(a, b, (((0,), (0,)), ((), ())), preferred_element_type=F32)


def ntdot(a, b):
    return lax.dot_general(a, b, (((1,), (1,)), ((), ())), preferred_element_type=F32)


def kernel(
    tab_hbm, sf_hbm, own_hbm, row_hbm, imp_hbm, w_hbm, o_self, o_w, o_t,
    tab, sf, own_in, row_in, imp_in,
    t_all, qi, sf_all, ps_out, ps_in, pooled, parts, gsend, grecv, hot, id_b, cand, w2, hot_in, gx_out, gx_in,
    at_hi, at_lo, cand_hi, cand_lo,
    wf, wtop, wbot, rx, rw, ry, half_out, half_in, face_out, face_in, line_out, line_in,
    sems, wsem,
):
    s = lax.axis_index("shard")
    x = lax.axis_index("rep")
    c = s & 1
    b = s >> 1
    z = b >> 2
    y = b & (NY - 1)
    e = y * NX + x
    partner = (b * 2 + 1 - c, x)

    def on_line(off):
        other = (z + off) & (NZ - 1)
        return other, ((other * NY + y) * 2 + c, x)

    def on_face(off):
        other = (e + off) & (NE - 1)
        return other, ((z * NY + (other >> 2)) * 2 + c, (other & (NX - 1)))

    def send(src, dst, row, to):
        pltpu.make_async_remote_copy(
            src_ref=src, dst_ref=dst, send_sem=sems.at[row, 0], recv_sem=sems.at[row, 1],
            device_id=to, device_id_type=MESH,
        ).start()

    def done(ref, row):
        return pltpu.make_async_remote_copy(
            src_ref=ref, dst_ref=ref, send_sem=sems.at[row, 0], recv_sem=sems.at[row, 1],
            device_id=partner, device_id_type=MESH,
        )

    def each(n, body):
        def step(i, carry):
            body(i)
            return carry
        lax.fori_loop(1, n, step, 0)

    zcol = pl.ds(pl.multiple_of(z * L, L), L)
    loads = [
        pltpu.make_async_copy(w_hbm.at[pl.ds(1024, 1024), zcol], wf, wsem.at[0]),
        pltpu.make_async_copy(w_hbm.at[pl.ds(0, 1024), :], wtop, wsem.at[1]),
        pltpu.make_async_copy(w_hbm.at[pl.ds(1024, 1024), :], wbot, wsem.at[2]),
    ]
    small = [
        pltpu.make_async_copy(src, dst, wsem.at[3 + i])
        for i, (src, dst) in enumerate((
            (own_hbm, own_in), (row_hbm, row_in), (imp_hbm, imp_in), (tab_hbm, tab), (sf_hbm, sf)))
    ]
    for load in small + loads:
        load.start()

    bar = pltpu.get_barrier_semaphore()

    def greet(to):
        pl.semaphore_signal(bar, inc=1, device_id=to, device_id_type=MESH)

    each(NZ, lambda i: greet(on_line(i)[1]))
    each(NE, lambda i: greet(on_face(i)[1]))
    greet(partner)
    small[3].wait()
    t_all[c, b] = tab[:, zcol]
    pl.semaphore_wait(bar, NZ - 1 + NE - 1 + 1)

    for k in (4, 3, 5, 2, 6, 1, 7):
        to_z = (z - k) & (NZ - 1)
        cols = pl.ds(pl.multiple_of(to_z * L, L), L)
        send(tab.at[:, cols], t_all.at[c, b], TZ_ + k, ((to_z * NY + y) * 2 + c, x))

    def pass_on(k):
        at = t_all.at[c, ((z + k) & (NZ - 1)) * NY + y]
        for dy in range(1, NY):
            send(at, at, TY_ + k, ((z * NY + ((y + dy) & (NY - 1))) * 2 + c, x))
        send(at, at, TP_, partner)

    pass_on(0)
    for load in small[:3]:
        load.wait()
    own = own_in[...]
    at = (own & 1) * HALF + (own >> 1) * 32 + row_in[...]
    qi[z] = jnp.zeros((Q, L), jnp.int32)
    qi[z, :, 0:K + C] = at
    qi[z, :, K + C:2 * K + C] = imp_in[...]
    each(NZ, lambda i: send(qi.at[z], qi.at[z], QI_, on_line(i)[1]))
    for k in (1, 7, 2, 6, 3, 5, 4):
        done(t_all.at[c, b], TZ_ + k).wait_recv()
        pass_on(k)

    small[4].wait()
    loads[1].wait()
    own_pre = jnp.dot(sf[...], wtop[...], preferred_element_type=F32)
    for f in range(NZ):
        ps_out[f] = own_pre[:, f * L:(f + 1) * L]
    each(NZ, lambda i: send(ps_out.at[on_line(i)[0]], ps_in.at[z], PS_, on_line(i)[1]))
    ps_in[z] = ps_out[z]
    own_self = sf[...].astype(F32)
    sf_all[z] = jnp.concatenate([own_self[:, :512], own_self[:, 512:]], axis=0).astype(BF16)
    each(NZ, lambda i: send(sf_all.at[z], sf_all.at[z], SF_, on_line(i)[1]))

    done(qi.at[pl.ds(0, NZ - 1)], QI_).wait_recv()
    ids = qi[...].reshape(G, L)
    imp = ids.astype(F32)
    lane = lax.broadcasted_iota(jnp.int32, (G, L), 1)
    query = lax.broadcasted_iota(jnp.int32, (G, L), 0) & (Q - 1)
    weighed = (lane >= K + C) & (lane < 2 * K + C)
    inv = 1.0 / jnp.sum(jnp.where(weighed, imp, 0.0), axis=1, keepdims=True)
    ids_hi = (ids >> 7) * Q + query
    ids_lo = ids & (L - 1)

    def spread(values, k):
        return jnp.broadcast_to(values[:, k:k + 1], (G, L))

    def pair(one, two):
        both = jnp.concatenate([one.reshape(NZ, Q, L), two.reshape(NZ, Q, L)], axis=1)
        return both.astype(BF16)

    def hit(values, k, weight=1.0):
        return jnp.where(spread(values, k) == lane, weight, 0.0)

    def outer(out, hi, lo):
        for m in range(NZ // 2):
            one = tdot(hi[2 * m], lo[2 * m])
            two = tdot(hi[2 * m + 1], lo[2 * m + 1])
            for h in range(ITEMS // L):
                both = jnp.concatenate([one[h * Q:(h + 1) * Q], two[h * Q:(h + 1) * Q]], axis=0)
                out[2 * m * Q:2 * (m + 1) * Q, h * L:(h + 1) * L] = both.astype(BF16)

    for m in range(K // 2):
        k = 2 * m
        at_hi[:, k * Q:(k + 2) * Q] = pair(hit(ids_hi, k), hit(ids_hi, k + 1))
        at_lo[:, k * Q:(k + 2) * Q] = pair(
            hit(ids_lo, k, spread(imp, K + C + k)), hit(ids_lo, k + 1, spread(imp, K + C + k + 1)))
    outer(hot.at[0], at_hi, at_lo)

    for k in (0, 1, 7, 2, 6, 3, 5, 4):
        first = ((z + k) & (NZ - 1)) * NY
        done(t_all.at[c, pl.ds(first, NY - 1)], TY_ + k).wait_recv()
        for dy in range(1, NY):
            at = t_all.at[c, first + ((y + dy) & (NY - 1))]
            send(at, at, TP_, partner)
    done(t_all.at[1 - c], TP_).wait_recv()

    rows = t_all[...].reshape(ITEMS, L)
    mine = jnp.dot(hot[0], rows, preferred_element_type=F32) * inv
    pooled[z] = mine.astype(BF16)
    each(NZ, lambda i: send(pooled.at[z], pooled.at[z], PO_, on_line(i)[1]))
    half = pl.ds(pl.multiple_of(c * HALF, HALF), HALF)
    other = pl.ds(pl.multiple_of((1 - c) * HALF, HALF), HALF)
    send(hot.at[0, :, other], hot_in, HP_, partner)
    for k in range(C):
        id_b[k] = spread(ids, K + k)

    def hot_chunk(h, carry):
        here = lane + h * L
        cols = pl.ds(pl.multiple_of(h * L, L), L)
        for k in range(C):
            hot[1 + k, :, cols] = jnp.where(id_b[k] == here, 1.0, 0.0).astype(BF16)
        return carry

    lax.fori_loop(0, ITEMS // L, hot_chunk, 0)
    cand[...] = jnp.dot(
        hot[1:1 + C].reshape(C * G, ITEMS), rows, preferred_element_type=F32
    ).reshape(C, G, L)

    zero = jnp.zeros((G, L), F32)
    for m in range((C + 1) // 2):
        k = K + 2 * m
        last = zero if 2 * m + 1 == C else hit(ids_hi, k + 1)
        cand_hi[:, 2 * m * Q:(2 * m + 2) * Q] = pair(hit(ids_hi, k), last)
    loads[0].wait()
    done(pooled.at[pl.ds(0, NZ - 1)], PO_).wait_recv()
    pool_all = jnp.concatenate([pooled[f] for f in range(NZ)], axis=1)
    done(ps_in.at[pl.ds(0, NZ - 1)], PS_).wait_recv()
    pre = ps_in[...].reshape(G, L) + jnp.dot(pool_all, wf[...], preferred_element_type=F32)
    gate = jax.nn.sigmoid(pre)
    act = pre * gate
    place = 32 * lax.rem(lax.div(lax.broadcasted_iota(jnp.int32, (G, L), 0), Q), 4)
    where_at = lane - place
    acc = jnp.where(where_at == C, jnp.sum(act * act, axis=1, keepdims=True), 0.0)
    for k in range(C):
        acc = jnp.where(where_at == k, jnp.sum(act * cand[k], axis=1, keepdims=True), acc)
    acc = acc.reshape(2, 4, Q, L)
    parts[z] = (acc[:, 0] + acc[:, 1] + acc[:, 2] + acc[:, 3]).reshape(2 * Q, L)
    each(NZ, lambda i: send(parts.at[z], parts.at[z], PC_, on_line(i)[1]))
    done(parts.at[pl.ds(0, NZ - 1)], PC_).wait_recv()
    total = parts[0]
    for f in range(1, NZ):
        total = total + parts[f]
    sums = jnp.concatenate(
        [total[(j // 4) * Q:(j // 4 + 1) * Q, 32 * (j % 4):32 * (j % 4) + 32] for j in range(NZ)],
        axis=0,
    )
    norm = jnp.sqrt(sums[:, C:C + 1] + EPS)
    score = sums / norm
    lane32 = lax.broadcasted_iota(jnp.int32, (G, 32), 1)
    negative = (lane32 >= 1) & (lane32 < C)
    slope = jnp.where(negative, jax.nn.sigmoid(score - score[:, 0:1] + MARGIN), 0.0)
    slope_sum = jnp.sum(slope, axis=1, keepdims=True)
    coef = jnp.where(lane32 == 0, -slope_sum, slope)
    along = jnp.sum(coef * score, axis=1, keepdims=True)
    grad_unit = jnp.zeros((G, L), F32)
    for k in range(C):
        grad_unit = grad_unit + spread(coef, k) * cand[k]
    unit = act / norm
    grad_act = (grad_unit - unit * along) / norm
    grad_pre = grad_act * gate * (1.0 + pre * (1.0 - gate))
    gp16 = grad_pre.astype(BF16)
    gp32 = gp16.astype(F32)

    def swap(n, half_of):
        for k in range(NE):
            half_out[n, k] = half_of(1 - c, k // NX, k % NX).reshape(NZ * Q, L).astype(BF16)
        send(half_out.at[n], half_in.at[n], HALF_ + n, partner)

    def scatter(n, half_of):
        done(half_in.at[n], HALF_ + n).wait_recv()
        for k in range(NE):
            own = half_of(c, k // NX, k % NX).reshape(NZ * Q, L)
            face_out[n, k] = (own + half_in[n, k].astype(F32)).astype(BF16)
        face_in[n, e] = face_out[n, e]

    PART = NZ // 2 * Q

    def spread_out(n, part):
        rows_at = pl.ds(part * PART, PART)
        each(NE, lambda i: send(
            face_out.at[n, on_face(i)[0], rows_at], face_in.at[n, e, rows_at],
            FACE_ + 2 * n + part, on_face(i)[1]))

    def half_w(core, yy, xx):
        return rw[:, yy, core, xx]

    def half_y(core, yy, xx):
        return ry[core, :, yy, xx]

    gx_out[...] = (gp32 * inv).astype(BF16)
    send(gx_out, gx_in, GX_, partner)

    for m in range((C + 1) // 2):
        k = 2 * m
        last = zero if k + 1 == C else hit(ids_lo, K + k + 1, spread(coef, k + 1))
        cand_lo[:, k * Q:(k + 2) * Q] = pair(hit(ids_lo, K + k, spread(coef, k)), last)
    outer(w2, cand_hi, cand_lo)
    ry[...] = tdot(w2[...], unit.astype(BF16)).reshape(2, NZ, NY, NX, Q, L)
    swap(1, half_y)
    done(hot_in, HP_).wait_recv()
    mine_x = tdot(hot[0, :, half], gx_out[...])
    done(gx_in, GX_).wait_recv()
    rx[...] = (mine_x + tdot(hot_in[...], gx_in[...])).reshape(NZ, NY, NX, Q, L)
    for k in range(NE):
        face_out[0, k] = rx[:, k // NX, k % NX].reshape(NZ * Q, L).astype(BF16)
    face_in[0, e] = face_out[0, e]
    spread_out(0, 0)

    done(sf_all.at[pl.ds(0, NZ - 1)], SF_).wait_recv()
    self2 = sf_all[...].reshape(2 * G, 512)
    blank = jnp.zeros((Q, L), F32)
    pieces = []
    for j in range(NZ):
        part = gp32[j * Q:(j + 1) * Q]
        pieces.append(jnp.concatenate([part, blank], axis=1))
        pieces.append(jnp.concatenate([blank, part], axis=1))
    gp2 = jnp.concatenate(pieces, axis=0).astype(BF16)
    gw_self = tdot(self2, gp2)
    rw[0:2] = gw_self[:, :L].reshape(2, NY, 2, NX, Q, L)
    rw[2:4] = gw_self[:, L:].reshape(2, NY, 2, NX, Q, L)
    rw[4:8] = tdot(pool_all, gp16).reshape(4, NY, 2, NX, Q, L)
    swap(2, half_w)
    scatter(1, half_y)
    spread_out(1, 0)
    spread_out(0, 1)

    gsend[...] = gp32.reshape(NZ, Q, L)
    each(NZ, lambda i: send(gsend.at[on_line(i)[0]], grecv.at[z], GP_, on_line(i)[1]))
    grecv[z] = gsend[z]
    scatter(2, half_w)
    spread_out(2, 0)
    spread_out(1, 1)
    spread_out(2, 1)

    done(grecv.at[pl.ds(0, NZ - 1)], GP_).wait_recv()
    gp_own = jnp.concatenate([grecv[f] for f in range(NZ)], axis=1).astype(BF16)
    o_self[...] = ntdot(gp_own, wtop[...])

    def finish(n, part):
        rows_at = pl.ds(part * PART, PART)
        done(face_in.at[n, pl.ds(0, NE - 1), rows_at], FACE_ + 2 * n + part).wait_recv()
        acc = face_in[n, 0, rows_at].astype(F32)
        for k in range(1, NE):
            acc = acc + face_in[n, k, rows_at].astype(F32)
        first = part * (NZ // 2)
        line_out[n, first:first + NZ // 2] = acc.reshape(NZ // 2, Q, L)
        for to_z in range(first, first + NZ // 2):
            @pl.when(z == to_z)
            def _():
                line_in[n, to_z] = line_out[n, to_z]

            @pl.when(z != to_z)
            def _():
                send(line_out.at[n, to_z], line_in.at[n, z], LINE_ + n, ((to_z * NY + y) * 2 + c, x))

    def row_sums(n):
        done(line_in.at[n, pl.ds(0, NZ - 1)], LINE_ + n).wait_recv()
        return jnp.concatenate([line_in[n, f] for f in range(NZ)], axis=1)

    for part in range(2):
        for n in range(3):
            finish(n, part)
    before = row_sums(0)
    rest = before - before.astype(BF16).astype(F32)
    loads[2].wait()
    after = ntdot(jnp.concatenate([before, rest], axis=0).astype(BF16), wbot[...])
    o_t[...] = after[0:Q] + after[Q:2 * Q] + row_sums(1)
    o_w[...] = row_sums(2)

    for ref, row in (
        (qi.at[pl.ds(0, NZ - 1)], QI_), (sf_all.at[pl.ds(0, NZ - 1)], SF_),
        (t_all.at[c], TP_), (pooled.at[pl.ds(0, NZ - 1)], PO_),
        (parts.at[pl.ds(0, NZ - 1)], PC_), (gsend.at[pl.ds(0, NZ - 1)], GP_),
        (ps_out.at[pl.ds(0, NZ - 1)], PS_), (hot.at[0, :, other], HP_), (gx_out, GX_),
    ):
        done(ref, row).wait_send()
    for k in range(NZ):
        if k:
            done(t_all.at[c, b], TZ_ + k).wait_send()
        done(t_all.at[c, pl.ds(0, NY - 1)], TY_ + k).wait_send()
    for n in range(3):
        if n:
            done(half_out.at[n], HALF_ + n).wait_send()
        for part in range(2):
            rows_at = pl.ds(part * PART, PART)
            done(face_out.at[n, pl.ds(0, NE - 1), rows_at], FACE_ + 2 * n + part).wait_send()
        done(line_out.at[n, pl.ds(0, NZ - 1)], LINE_ + n).wait_send()


def hand_over(a, b, c, to_a, to_b, to_c):
    to_a[...] = a[...]
    to_b[...] = b[...]
    to_c[...] = c[...]


def local(table, self_feat, weight, owners, item_rows, importance):
    vmem = pl.BlockSpec(memory_space=pltpu.VMEM)
    hbm = pl.BlockSpec(memory_space=pl.ANY)
    out = jax.ShapeDtypeStruct((Q, 1024), F32)
    V = pltpu.VMEM
    grads = pl.pallas_call(
        kernel,
        out_shape=(out, out, out),
        in_specs=[hbm] * 6,
        out_specs=(vmem, vmem, vmem),
        scratch_shapes=[
            V((32, 1024), BF16),
            V((Q, 1024), BF16),
            V((Q, K + C), jnp.int32),
            V((Q, K + C), jnp.int32),
            V((Q, K), jnp.int32),
            V((2, NB, 32, L), BF16),
            V((NZ, Q, L), jnp.int32),
            V((NZ, 2 * Q, 512), BF16),
            V((NZ, Q, L), F32),
            V((NZ, Q, L), F32),
            V((NZ, G, L), BF16),
            V((NZ, 2 * Q, L), F32),
            V((NZ, Q, L), F32),
            V((NZ, Q, L), F32),
            V((1 + C, G, ITEMS), BF16),
            V((C, G, L), jnp.int32),
            V((C, G, L), F32),
            V((G, ITEMS), BF16),
            V((G, HALF), BF16),
            V((G, L), BF16),
            V((G, L), BF16),
            V((NZ, K * Q, L), BF16),
            V((NZ, K * Q, L), BF16),
            V((NZ, (C + 1) * Q, L), BF16),
            V((NZ, (C + 1) * Q, L), BF16),
            V((1024, L), BF16),
            V((1024, 1024), BF16),
            V((1024, 1024), BF16),
            V((NZ, NY, NX, Q, L), F32),
            V((NZ, NY, 2, NX, Q, L), F32),
            V((2, NZ, NY, NX, Q, L), F32),
            V((3, NE, G, L), BF16),
            V((3, NE, G, L), BF16),
            V((3, NE, G, L), BF16),
            V((3, NE, G, L), BF16),
            V((3, NZ, Q, L), F32),
            V((3, NZ, Q, L), F32),
            pltpu.SemaphoreType.DMA((37, 2)),
            pltpu.SemaphoreType.DMA((8,)),
        ],
        compiler_params=pltpu.CompilerParams(
            collective_id=0, has_side_effects=True, vmem_limit_bytes=62 * 1024 * 1024
        ),
    )(table, self_feat, owners.reshape(Q, K + C), item_rows, importance, weight)
    return pl.pallas_call(
        hand_over, out_shape=(out, out, out), in_specs=[vmem] * 3, out_specs=(vmem,) * 3
    )(*grads)


def solution(mesh):
    both = ("shard", "rep")
    in_specs = (
        P("shard", None), P(both, None), P(), P(both, None, None), P(both, None), P(both, None),
    )
    out_specs = (P(both, None), P(both, None), P(both, None))
    return jax.shard_map(local, mesh=mesh, in_specs=in_specs, out_specs=out_specs, check_vma=False)
```

```python
import jax
import jax.numpy as jnp
from jax import lax
from jax.experimental import pallas as pl
from jax.experimental.pallas import tpu as pltpu
from jax.sharding import PartitionSpec as P

MESH = pl.DeviceIdType.MESH
MARGIN = 0.5
EPS = 1e-06
K = 50
C = 17
NZ, NY, NX = 8, 4, 4
NB = NZ * NY
NE = NY * NX
Q = 8
G = NZ * Q
L = 128
ITEMS = 2048
HALF = ITEMS // 2
F32, BF16 = jnp.float32, jnp.bfloat16
QI_, SF_, TP_, PO_, PC_, GP_, PS_, HP_, GX_ = range(9)
HALF_, LINE_, FACE_ = 9, 12, 15
TZ_, TY_ = 21, 29


def tdot(a, b):
    return lax.dot_general(a, b, (((0,), (0,)), ((), ())), preferred_element_type=F32)


def ntdot(a, b):
    return lax.dot_general(a, b, (((1,), (1,)), ((), ())), preferred_element_type=F32)


def kernel(
    tab_hbm, sf_hbm, own_hbm, row_hbm, imp_hbm, w_hbm, o_self, o_w, o_t,
    tab, sf, own_in, row_in, imp_in,
    t_all, qi, sf_all, ps_out, ps_in, pooled, parts, gsend, grecv, hot, id_b, cand, w2, hot_in, gx_out, gx_in,
    at_hi, at_lo, cand_hi, cand_lo,
    wf, wtop, wbot, rx, rw, ry, half_out, half_in, face_out, face_in, line_out, line_in,
    sems, wsem,
):
    s = lax.axis_index("shard")
    x = lax.axis_index("rep")
    c = s & 1
    b = s >> 1
    z = b >> 2
    y = b & (NY - 1)
    e = y * NX + x
    partner = (b * 2 + 1 - c, x)

    def on_line():
        for k in (4, 3, 5, 2, 6, 1, 7):
            other = (z + k) & (NZ - 1)
            yield other, ((other * NY + y) * 2 + c, x)

    def on_face():
        steps = [(dy, dx) for dy in range(NY) for dx in range(NX)][1:]
        for dy, dx in sorted(steps, key=lambda step: -min(step[0], 4 - step[0]) - min(step[1], 4 - step[1])):
            yy, xx = (y + dy) & (NY - 1), (x + dx) & (NX - 1)
            yield yy * NX + xx, ((z * NY + yy) * 2 + c, xx)

    def send(src, dst, row, to):
        pltpu.make_async_remote_copy(
            src_ref=src, dst_ref=dst, send_sem=sems.at[row, 0], recv_sem=sems.at[row, 1],
            device_id=to, device_id_type=MESH,
        ).start()

    def done(ref, row):
        return pltpu.make_async_remote_copy(
            src_ref=ref, dst_ref=ref, send_sem=sems.at[row, 0], recv_sem=sems.at[row, 1],
            device_id=partner, device_id_type=MESH,
        )

    zcol = pl.ds(pl.multiple_of(z * L, L), L)
    loads = [
        pltpu.make_async_copy(w_hbm.at[pl.ds(1024, 1024), zcol], wf, wsem.at[0]),
        pltpu.make_async_copy(w_hbm.at[pl.ds(0, 1024), :], wtop, wsem.at[1]),
        pltpu.make_async_copy(w_hbm.at[pl.ds(1024, 1024), :], wbot, wsem.at[2]),
    ]
    small = [
        pltpu.make_async_copy(src, dst, wsem.at[3 + i])
        for i, (src, dst) in enumerate((
            (own_hbm, own_in), (row_hbm, row_in), (imp_hbm, imp_in), (tab_hbm, tab), (sf_hbm, sf)))
    ]
    for load in small + loads:
        load.start()

    bar = pltpu.get_barrier_semaphore()

    def greet(to):
        pl.semaphore_signal(bar, inc=1, device_id=to, device_id_type=MESH)

    for _, to in [*on_line(), *on_face()]:
        greet(to)
    greet(partner)
    small[3].wait()
    t_all[c, b] = tab[:, zcol]
    pl.semaphore_wait(bar, NZ - 1 + NE - 1 + 1)

    for k in (4, 3, 5, 2, 6, 1, 7):
        to_z = (z - k) & (NZ - 1)
        cols = pl.ds(pl.multiple_of(to_z * L, L), L)
        send(tab.at[:, cols], t_all.at[c, b], TZ_ + k, ((to_z * NY + y) * 2 + c, x))

    def pass_on(k):
        at = t_all.at[c, ((z + k) & (NZ - 1)) * NY + y]
        for dy in range(1, NY):
            send(at, at, TY_ + k, ((z * NY + ((y + dy) & (NY - 1))) * 2 + c, x))
        send(at, at, TP_, partner)

    pass_on(0)
    for load in small[:3]:
        load.wait()
    own = own_in[...]
    at = (own & 1) * HALF + (own >> 1) * 32 + row_in[...]
    qi[z] = jnp.zeros((Q, L), jnp.int32)
    qi[z, :, 0:K + C] = at
    qi[z, :, K + C:2 * K + C] = imp_in[...]
    for _, to in on_line():
        send(qi.at[z], qi.at[z], QI_, to)
    for k in (1, 7, 2, 6, 3, 5, 4):
        done(t_all.at[c, b], TZ_ + k).wait_recv()
        pass_on(k)

    small[4].wait()
    loads[1].wait()
    own_pre = jnp.dot(sf[...], wtop[...], preferred_element_type=F32)
    for f in range(NZ):
        ps_out[f] = own_pre[:, f * L:(f + 1) * L]
    for other, to in on_line():
        send(ps_out.at[other], ps_in.at[z], PS_, to)
    ps_in[z] = ps_out[z]
    own_self = sf[...].astype(F32)
    sf_all[z] = jnp.concatenate([own_self[:, :512], own_self[:, 512:]], axis=0).astype(BF16)
    for _, to in on_line():
        send(sf_all.at[z], sf_all.at[z], SF_, to)

    done(qi.at[pl.ds(0, NZ - 1)], QI_).wait_recv()
    ids = qi[...].reshape(G, L)
    imp = ids.astype(F32)
    lane = lax.broadcasted_iota(jnp.int32, (G, L), 1)
    query = lax.broadcasted_iota(jnp.int32, (G, L), 0) & (Q - 1)
    weighed = (lane >= K + C) & (lane < 2 * K + C)
    inv = 1.0 / jnp.sum(jnp.where(weighed, imp, 0.0), axis=1, keepdims=True)
    ids_hi = (ids >> 7) * Q + query
    ids_lo = ids & (L - 1)

    def spread(values, k):
        return jnp.broadcast_to(values[:, k:k + 1], (G, L))

    def pair(one, two):
        both = jnp.concatenate([one.reshape(NZ, Q, L), two.reshape(NZ, Q, L)], axis=1)
        return both.astype(BF16)

    def hit(values, k, weight=1.0):
        return jnp.where(spread(values, k) == lane, weight, 0.0)

    def outer(out, hi, lo):
        for m in range(NZ // 2):
            one = tdot(hi[2 * m], lo[2 * m])
            two = tdot(hi[2 * m + 1], lo[2 * m + 1])
            for h in range(ITEMS // L):
                both = jnp.concatenate([one[h * Q:(h + 1) * Q], two[h * Q:(h + 1) * Q]], axis=0)
                out[2 * m * Q:2 * (m + 1) * Q, h * L:(h + 1) * L] = both.astype(BF16)

    for m in range(K // 2):
        k = 2 * m
        at_hi[:, k * Q:(k + 2) * Q] = pair(hit(ids_hi, k), hit(ids_hi, k + 1))
        at_lo[:, k * Q:(k + 2) * Q] = pair(
            hit(ids_lo, k, spread(imp, K + C + k)), hit(ids_lo, k + 1, spread(imp, K + C + k + 1)))
    outer(hot.at[0], at_hi, at_lo)

    for k in (0, 1, 7, 2, 6, 3, 5, 4):
        first = ((z + k) & (NZ - 1)) * NY
        done(t_all.at[c, pl.ds(first, NY - 1)], TY_ + k).wait_recv()
        for dy in range(1, NY):
            at = t_all.at[c, first + ((y + dy) & (NY - 1))]
            send(at, at, TP_, partner)
    done(t_all.at[1 - c], TP_).wait_recv()

    rows = t_all[...].reshape(ITEMS, L)
    mine = jnp.dot(hot[0], rows, preferred_element_type=F32) * inv
    pooled[z] = mine.astype(BF16)
    for _, to in on_line():
        send(pooled.at[z], pooled.at[z], PO_, to)
    half = pl.ds(pl.multiple_of(c * HALF, HALF), HALF)
    away = pl.ds(pl.multiple_of((1 - c) * HALF, HALF), HALF)
    send(hot.at[0, :, away], hot_in, HP_, partner)
    for k in range(C):
        id_b[k] = spread(ids, K + k)

    def hot_chunk(h, carry):
        here = lane + h * L
        cols = pl.ds(pl.multiple_of(h * L, L), L)
        for k in range(C):
            hot[1 + k, :, cols] = jnp.where(id_b[k] == here, 1.0, 0.0).astype(BF16)
        return carry

    lax.fori_loop(0, ITEMS // L, hot_chunk, 0)
    cand[...] = jnp.dot(
        hot[1:1 + C].reshape(C * G, ITEMS), rows, preferred_element_type=F32
    ).reshape(C, G, L)

    zero = jnp.zeros((G, L), F32)
    for m in range((C + 1) // 2):
        k = K + 2 * m
        last = zero if 2 * m + 1 == C else hit(ids_hi, k + 1)
        cand_hi[:, 2 * m * Q:(2 * m + 2) * Q] = pair(hit(ids_hi, k), last)
    loads[0].wait()
    done(pooled.at[pl.ds(0, NZ - 1)], PO_).wait_recv()
    pool_all = jnp.concatenate([pooled[f] for f in range(NZ)], axis=1)
    done(ps_in.at[pl.ds(0, NZ - 1)], PS_).wait_recv()
    pre = ps_in[...].reshape(G, L) + jnp.dot(pool_all, wf[...], preferred_element_type=F32)
    gate = jax.nn.sigmoid(pre)
    act = pre * gate
    place = 32 * lax.rem(lax.div(lax.broadcasted_iota(jnp.int32, (G, L), 0), Q), 4)
    where_at = lane - place
    acc = jnp.where(where_at == C, jnp.sum(act * act, axis=1, keepdims=True), 0.0)
    for k in range(C):
        acc = jnp.where(where_at == k, jnp.sum(act * cand[k], axis=1, keepdims=True), acc)
    acc = acc.reshape(2, 4, Q, L)
    parts[z] = (acc[:, 0] + acc[:, 1] + acc[:, 2] + acc[:, 3]).reshape(2 * Q, L)
    for _, to in on_line():
        send(parts.at[z], parts.at[z], PC_, to)
    done(parts.at[pl.ds(0, NZ - 1)], PC_).wait_recv()
    total = parts[0]
    for f in range(1, NZ):
        total = total + parts[f]
    sums = jnp.concatenate(
        [total[(j // 4) * Q:(j // 4 + 1) * Q, 32 * (j % 4):32 * (j % 4) + 32] for j in range(NZ)],
        axis=0,
    )
    norm = jnp.sqrt(sums[:, C:C + 1] + EPS)
    score = sums / norm
    lane32 = lax.broadcasted_iota(jnp.int32, (G, 32), 1)
    negative = (lane32 >= 1) & (lane32 < C)
    slope = jnp.where(negative, jax.nn.sigmoid(score - score[:, 0:1] + MARGIN), 0.0)
    slope_sum = jnp.sum(slope, axis=1, keepdims=True)
    coef = jnp.where(lane32 == 0, -slope_sum, slope)
    along = jnp.sum(coef * score, axis=1, keepdims=True)
    grad_unit = jnp.zeros((G, L), F32)
    for k in range(C):
        grad_unit = grad_unit + spread(coef, k) * cand[k]
    unit = act / norm
    grad_act = (grad_unit - unit * along) / norm
    grad_pre = grad_act * gate * (1.0 + pre * (1.0 - gate))
    gp16 = grad_pre.astype(BF16)
    gp32 = gp16.astype(F32)

    def swap(n, half_of):
        for k in range(NE):
            half_out[n, k] = half_of(1 - c, k // NX, k % NX).reshape(NZ * Q, L).astype(BF16)
        send(half_out.at[n], half_in.at[n], HALF_ + n, partner)

    def scatter(n, half_of):
        done(half_in.at[n], HALF_ + n).wait_recv()
        for k in range(NE):
            own = half_of(c, k // NX, k % NX).reshape(NZ * Q, L)
            face_out[n, k] = (own + half_in[n, k].astype(F32)).astype(BF16)
        face_in[n, e] = face_out[n, e]

    PART = NZ // 2 * Q

    def spread_out(n, part):
        rows_at = pl.ds(part * PART, PART)
        for other, to in on_face():
            send(face_out.at[n, other, rows_at], face_in.at[n, e, rows_at], FACE_ + 2 * n + part, to)

    def half_w(core, yy, xx):
        return rw[:, yy, core, xx]

    def half_y(core, yy, xx):
        return ry[core, :, yy, xx]

    gx_out[...] = (gp32 * inv).astype(BF16)
    send(gx_out, gx_in, GX_, partner)

    for m in range((C + 1) // 2):
        k = 2 * m
        last = zero if k + 1 == C else hit(ids_lo, K + k + 1, spread(coef, k + 1))
        cand_lo[:, k * Q:(k + 2) * Q] = pair(hit(ids_lo, K + k, spread(coef, k)), last)
    outer(w2, cand_hi, cand_lo)
    ry[...] = tdot(w2[...], unit.astype(BF16)).reshape(2, NZ, NY, NX, Q, L)
    swap(1, half_y)
    done(sf_all.at[pl.ds(0, NZ - 1)], SF_).wait_recv()
    self2 = sf_all[...].reshape(2 * G, 512)
    blank = jnp.zeros((Q, L), F32)
    pieces = []
    for j in range(NZ):
        part = gp32[j * Q:(j + 1) * Q]
        pieces.append(jnp.concatenate([part, blank], axis=1))
        pieces.append(jnp.concatenate([blank, part], axis=1))
    gp2 = jnp.concatenate(pieces, axis=0).astype(BF16)
    gw_self = tdot(self2, gp2)
    rw[0:2] = gw_self[:, :L].reshape(2, NY, 2, NX, Q, L)
    rw[2:4] = gw_self[:, L:].reshape(2, NY, 2, NX, Q, L)
    rw[4:8] = tdot(pool_all, gp16).reshape(4, NY, 2, NX, Q, L)
    swap(2, half_w)
    done(hot_in, HP_).wait_recv()
    mine_x = tdot(hot[0, :, half], gx_out[...])
    done(gx_in, GX_).wait_recv()
    rx[...] = (mine_x + tdot(hot_in[...], gx_in[...])).reshape(NZ, NY, NX, Q, L)
    for k in range(NE):
        face_out[0, k] = rx[:, k // NX, k % NX].reshape(NZ * Q, L).astype(BF16)
    face_in[0, e] = face_out[0, e]
    spread_out(0, 0)
    scatter(1, half_y)
    spread_out(1, 0)

    gsend[...] = gp32.reshape(NZ, Q, L)
    for other, to in on_line():
        send(gsend.at[other], grecv.at[z], GP_, to)
    grecv[z] = gsend[z]
    scatter(2, half_w)
    spread_out(2, 0)
    spread_out(0, 1)
    spread_out(1, 1)
    spread_out(2, 1)

    done(grecv.at[pl.ds(0, NZ - 1)], GP_).wait_recv()
    gp_own = jnp.concatenate([grecv[f] for f in range(NZ)], axis=1).astype(BF16)
    o_self[...] = ntdot(gp_own, wtop[...])

    def finish(n, part):
        rows_at = pl.ds(part * PART, PART)
        done(face_in.at[n, pl.ds(0, NE - 1), rows_at], FACE_ + 2 * n + part).wait_recv()
        acc = face_in[n, 0, rows_at].astype(F32)
        for k in range(1, NE):
            acc = acc + face_in[n, k, rows_at].astype(F32)
        first = part * (NZ // 2)
        line_out[n, first:first + NZ // 2] = acc.reshape(NZ // 2, Q, L)
        for to_z in range(first, first + NZ // 2):
            @pl.when(z == to_z)
            def _():
                line_in[n, to_z] = line_out[n, to_z]

            @pl.when(z != to_z)
            def _():
                send(line_out.at[n, to_z], line_in.at[n, z], LINE_ + n, ((to_z * NY + y) * 2 + c, x))

    def row_sums(n):
        done(line_in.at[n, pl.ds(0, NZ - 1)], LINE_ + n).wait_recv()
        return jnp.concatenate([line_in[n, f] for f in range(NZ)], axis=1)

    for part in range(2):
        for n in range(3):
            finish(n, part)
    before = row_sums(0)
    rest = before - before.astype(BF16).astype(F32)
    loads[2].wait()
    after = ntdot(jnp.concatenate([before, rest], axis=0).astype(BF16), wbot[...])
    o_t[...] = after[0:Q] + after[Q:2 * Q] + row_sums(1)
    o_w[...] = row_sums(2)

    for ref, row in (
        (qi.at[pl.ds(0, NZ - 1)], QI_), (sf_all.at[pl.ds(0, NZ - 1)], SF_),
        (t_all.at[c], TP_), (pooled.at[pl.ds(0, NZ - 1)], PO_),
        (parts.at[pl.ds(0, NZ - 1)], PC_), (gsend.at[pl.ds(0, NZ - 1)], GP_),
        (ps_out.at[pl.ds(0, NZ - 1)], PS_), (hot.at[0, :, away], HP_), (gx_out, GX_),
    ):
        done(ref, row).wait_send()
    for k in range(NZ):
        if k:
            done(t_all.at[c, b], TZ_ + k).wait_send()
        done(t_all.at[c, pl.ds(0, NY - 1)], TY_ + k).wait_send()
    for n in range(3):
        if n:
            done(half_out.at[n], HALF_ + n).wait_send()
        for part in range(2):
            rows_at = pl.ds(part * PART, PART)
            done(face_out.at[n, pl.ds(0, NE - 1), rows_at], FACE_ + 2 * n + part).wait_send()
        done(line_out.at[n, pl.ds(0, NZ - 1)], LINE_ + n).wait_send()


def hand_over(a, b, c, to_a, to_b, to_c):
    to_a[...] = a[...]
    to_b[...] = b[...]
    to_c[...] = c[...]


def local(table, self_feat, weight, owners, item_rows, importance):
    vmem = pl.BlockSpec(memory_space=pltpu.VMEM)
    hbm = pl.BlockSpec(memory_space=pl.ANY)
    out = jax.ShapeDtypeStruct((Q, 1024), F32)
    V = pltpu.VMEM
    grads = pl.pallas_call(
        kernel,
        out_shape=(out, out, out),
        in_specs=[hbm] * 6,
        out_specs=(vmem, vmem, vmem),
        scratch_shapes=[
            V((32, 1024), BF16),
            V((Q, 1024), BF16),
            V((Q, K + C), jnp.int32),
            V((Q, K + C), jnp.int32),
            V((Q, K), jnp.int32),
            V((2, NB, 32, L), BF16),
            V((NZ, Q, L), jnp.int32),
            V((NZ, 2 * Q, 512), BF16),
            V((NZ, Q, L), F32),
            V((NZ, Q, L), F32),
            V((NZ, G, L), BF16),
            V((NZ, 2 * Q, L), F32),
            V((NZ, Q, L), F32),
            V((NZ, Q, L), F32),
            V((1 + C, G, ITEMS), BF16),
            V((C, G, L), jnp.int32),
            V((C, G, L), F32),
            V((G, ITEMS), BF16),
            V((G, HALF), BF16),
            V((G, L), BF16),
            V((G, L), BF16),
            V((NZ, K * Q, L), BF16),
            V((NZ, K * Q, L), BF16),
            V((NZ, (C + 1) * Q, L), BF16),
            V((NZ, (C + 1) * Q, L), BF16),
            V((1024, L), BF16),
            V((1024, 1024), BF16),
            V((1024, 1024), BF16),
            V((NZ, NY, NX, Q, L), F32),
            V((NZ, NY, 2, NX, Q, L), F32),
            V((2, NZ, NY, NX, Q, L), F32),
            V((3, NE, G, L), BF16),
            V((3, NE, G, L), BF16),
            V((3, NE, G, L), BF16),
            V((3, NE, G, L), BF16),
            V((3, NZ, Q, L), F32),
            V((3, NZ, Q, L), F32),
            pltpu.SemaphoreType.DMA((37, 2)),
            pltpu.SemaphoreType.DMA((8,)),
        ],
        compiler_params=pltpu.CompilerParams(
            collective_id=0, has_side_effects=True, vmem_limit_bytes=62 * 1024 * 1024
        ),
    )(table, self_feat, owners.reshape(Q, K + C), item_rows, importance, weight)
    return pl.pallas_call(
        hand_over, out_shape=(out, out, out), in_specs=[vmem] * 3, out_specs=(vmem,) * 3
    )(*grads)


def solution(mesh):
    both = ("shard", "rep")
    in_specs = (
        P("shard", None), P(both, None), P(), P(both, None, None), P(both, None), P(both, None),
    )
    out_specs = (P(both, None), P(both, None), P(both, None))
    return jax.shard_map(local, mesh=mesh, in_specs=in_specs, out_specs=out_specs, check_vma=False)
```

```python
import jax
import jax.numpy as jnp
from jax import lax
from jax.experimental import pallas as pl
from jax.experimental.pallas import tpu as pltpu
from jax.sharding import PartitionSpec as P

MESH = pl.DeviceIdType.MESH
MARGIN = 0.5
EPS = 1e-06
K = 50
C = 17
NZ, NY, NX = 8, 4, 4
NB = NZ * NY
NE = NY * NX
Q = 8
G = NZ * Q
L = 128
ITEMS = 2048
HALF = ITEMS // 2
F32, BF16 = jnp.float32, jnp.bfloat16
PARTS = ((0, 4), (4, 8))
QI_, SF_, TP_, PO_, PC_, GP_, PS_, HP_, GX_, W2_, PB_, SB_ = range(12)
LINE_, FACE_ = 12, 15
TZ_, TY_ = 24, 32


def tdot(a, b):
    return lax.dot_general(a, b, (((0,), (0,)), ((), ())), preferred_element_type=F32)


def ntdot(a, b):
    return lax.dot_general(a, b, (((1,), (1,)), ((), ())), preferred_element_type=F32)


def kernel(
    tab_hbm, sf_hbm, own_hbm, row_hbm, imp_hbm, w_hbm, o_self, o_w, o_t,
    tab, sf, own_in, row_in, imp_in,
    t_all, qi, sf_all, ps_out, ps_in, pooled, parts, gsend, grecv, hot, id_b, cand, w2, hot_in, gx_out, gx_in,
    at_hi, at_lo, cand_hi, cand_lo,
    wf, wtop, wbot, rx, rw, ry, pool_in, self_in, w2_in, face_out, face_in, line_out, line_in,
    sems, wsem,
):
    s = lax.axis_index("shard")
    x = lax.axis_index("rep")
    c = s & 1
    b = s >> 1
    z = b >> 2
    y = b & (NY - 1)
    e = y * NX + x
    partner = (b * 2 + 1 - c, x)

    def on_line():
        for k in (4, 3, 5, 2, 6, 1, 7):
            other = (z + k) & (NZ - 1)
            yield other, ((other * NY + y) * 2 + c, x)

    def on_face():
        steps = [(dy, dx) for dy in range(NY) for dx in range(NX)][1:]
        for dy, dx in sorted(steps, key=lambda step: -min(step[0], 4 - step[0]) - min(step[1], 4 - step[1])):
            yy, xx = (y + dy) & (NY - 1), (x + dx) & (NX - 1)
            yield yy * NX + xx, ((z * NY + yy) * 2 + c, xx)

    def send(src, dst, row, to):
        pltpu.make_async_remote_copy(
            src_ref=src, dst_ref=dst, send_sem=sems.at[row, 0], recv_sem=sems.at[row, 1],
            device_id=to, device_id_type=MESH,
        ).start()

    def done(ref, row):
        return pltpu.make_async_remote_copy(
            src_ref=ref, dst_ref=ref, send_sem=sems.at[row, 0], recv_sem=sems.at[row, 1],
            device_id=partner, device_id_type=MESH,
        )

    zcol = pl.ds(pl.multiple_of(z * L, L), L)
    loads = [
        pltpu.make_async_copy(w_hbm.at[pl.ds(1024, 1024), zcol], wf, wsem.at[0]),
        pltpu.make_async_copy(w_hbm.at[pl.ds(0, 1024), :], wtop, wsem.at[1]),
        pltpu.make_async_copy(w_hbm.at[pl.ds(1024, 1024), :], wbot, wsem.at[2]),
    ]
    small = [
        pltpu.make_async_copy(src, dst, wsem.at[3 + i])
        for i, (src, dst) in enumerate((
            (own_hbm, own_in), (row_hbm, row_in), (imp_hbm, imp_in), (tab_hbm, tab), (sf_hbm, sf)))
    ]
    for load in small + loads:
        load.start()

    bar = pltpu.get_barrier_semaphore()

    def greet(to):
        pl.semaphore_signal(bar, inc=1, device_id=to, device_id_type=MESH)

    for _, to in [*on_line(), *on_face()]:
        greet(to)
    greet(partner)
    small[3].wait()
    t_all[c, b] = tab[:, zcol]
    pl.semaphore_wait(bar, NZ - 1 + NE - 1 + 1)

    for k in (4, 3, 5, 2, 6, 1, 7):
        to_z = (z - k) & (NZ - 1)
        cols = pl.ds(pl.multiple_of(to_z * L, L), L)
        send(tab.at[:, cols], t_all.at[c, b], TZ_ + k, ((to_z * NY + y) * 2 + c, x))

    def pass_on(k):
        at = t_all.at[c, ((z + k) & (NZ - 1)) * NY + y]
        for dy in (2, 1, 3):
            send(at, at, TY_ + k, ((z * NY + ((y + dy) & (NY - 1))) * 2 + c, x))
        send(at, at, TP_, partner)

    pass_on(0)
    for load in small[:3]:
        load.wait()
    own = own_in[...]
    at = (own & 1) * HALF + (own >> 1) * 32 + row_in[...]
    qi[z] = jnp.zeros((Q, L), jnp.int32)
    qi[z, :, 0:K + C] = at
    qi[z, :, K + C:2 * K + C] = imp_in[...]
    for _, to in on_line():
        send(qi.at[z], qi.at[z], QI_, to)
    for k in (1, 7, 2, 6, 3, 5, 4):
        done(t_all.at[c, b], TZ_ + k).wait_recv()
        pass_on(k)

    small[4].wait()
    loads[1].wait()
    own_pre = jnp.dot(sf[...], wtop[...], preferred_element_type=F32)
    for f in range(NZ):
        ps_out[f] = own_pre[:, f * L:(f + 1) * L]
    for other, to in on_line():
        send(ps_out.at[other], ps_in.at[z], PS_, to)
    ps_in[z] = ps_out[z]
    own_self = sf[...].astype(F32)
    sf_all[z] = jnp.concatenate([own_self[:, :512], own_self[:, 512:]], axis=0).astype(BF16)
    for _, to in on_line():
        send(sf_all.at[z], sf_all.at[z], SF_, to)

    done(qi.at[pl.ds(0, NZ - 1)], QI_).wait_recv()
    ids = qi[...].reshape(G, L)
    imp = ids.astype(F32)
    lane = lax.broadcasted_iota(jnp.int32, (G, L), 1)
    query = lax.broadcasted_iota(jnp.int32, (G, L), 0) & (Q - 1)
    weighed = (lane >= K + C) & (lane < 2 * K + C)
    inv = 1.0 / jnp.sum(jnp.where(weighed, imp, 0.0), axis=1, keepdims=True)
    ids_hi = (ids >> 7) * Q + query
    ids_lo = ids & (L - 1)

    def spread(values, k):
        return jnp.broadcast_to(values[:, k:k + 1], (G, L))

    def pair(one, two):
        both = jnp.concatenate([one.reshape(NZ, Q, L), two.reshape(NZ, Q, L)], axis=1)
        return both.astype(BF16)

    def hit(values, k, weight=1.0):
        return jnp.where(spread(values, k) == lane, weight, 0.0)

    def outer(out, hi, lo):
        for m in range(NZ // 2):
            one = tdot(hi[2 * m], lo[2 * m])
            two = tdot(hi[2 * m + 1], lo[2 * m + 1])
            for h in range(ITEMS // L):
                both = jnp.concatenate([one[h * Q:(h + 1) * Q], two[h * Q:(h + 1) * Q]], axis=0)
                out[2 * m * Q:2 * (m + 1) * Q, h * L:(h + 1) * L] = both.astype(BF16)

    for m in range(K // 2):
        k = 2 * m
        at_hi[:, k * Q:(k + 2) * Q] = pair(hit(ids_hi, k), hit(ids_hi, k + 1))
        at_lo[:, k * Q:(k + 2) * Q] = pair(
            hit(ids_lo, k, spread(imp, K + C + k)), hit(ids_lo, k + 1, spread(imp, K + C + k + 1)))
    outer(hot.at[0], at_hi, at_lo)

    for k in (0, 1, 7, 2, 6, 3, 5, 4):
        first = ((z + k) & (NZ - 1)) * NY
        done(t_all.at[c, pl.ds(first, NY - 1)], TY_ + k).wait_recv()
        for dy in range(1, NY):
            at = t_all.at[c, first + ((y + dy) & (NY - 1))]
            send(at, at, TP_, partner)
    done(t_all.at[1 - c], TP_).wait_recv()

    rows = t_all[...].reshape(ITEMS, L)
    mine = jnp.dot(hot[0], rows, preferred_element_type=F32) * inv
    pooled[z] = mine.astype(BF16)
    for _, to in on_line():
        send(pooled.at[z], pooled.at[z], PO_, to)
    half = pl.ds(pl.multiple_of(c * HALF, HALF), HALF)
    away = pl.ds(pl.multiple_of((1 - c) * HALF, HALF), HALF)
    send(hot.at[0, :, away], hot_in, HP_, partner)
    for k in range(C):
        id_b[k] = spread(ids, K + k)

    def hot_chunk(h, carry):
        here = lane + h * L
        cols = pl.ds(pl.multiple_of(h * L, L), L)
        for k in range(C):
            hot[1 + k, :, cols] = jnp.where(id_b[k] == here, 1.0, 0.0).astype(BF16)
        return carry

    lax.fori_loop(0, ITEMS // L, hot_chunk, 0)
    cand[...] = jnp.dot(
        hot[1:1 + C].reshape(C * G, ITEMS), rows, preferred_element_type=F32
    ).reshape(C, G, L)
    for k in range(1, C):
        cand[k] = cand[k] - cand[0]

    zero = jnp.zeros((G, L), F32)
    for m in range((C + 1) // 2):
        k = K + 2 * m
        last = zero if 2 * m + 1 == C else hit(ids_hi, k + 1)
        cand_hi[:, 2 * m * Q:(2 * m + 2) * Q] = pair(hit(ids_hi, k), last)
    loads[0].wait()
    done(pooled.at[pl.ds(0, NZ - 1)], PO_).wait_recv()
    pool_all = jnp.concatenate([pooled[f] for f in range(NZ)], axis=1)
    done(ps_in.at[pl.ds(0, NZ - 1)], PS_).wait_recv()
    pre = ps_in[...].reshape(G, L) + jnp.dot(pool_all, wf[...], preferred_element_type=F32)
    gate = jax.nn.sigmoid(pre)
    act = pre * gate
    sent_rows = pl.ds(0, Q + 1)
    row = lax.broadcasted_iota(jnp.int32, (G, L), 0)
    where_at = lane - (C - 1) * (row >> 3)
    acc = zero
    for k in range(1, C):
        acc = jnp.where(where_at == k - 1, jnp.sum(act * cand[k], axis=1, keepdims=True), acc)
    parts[z, 0:Q] = jnp.sum(acc.reshape(NZ, Q, L), axis=0)
    squares = jnp.sum(act * act, axis=1, keepdims=True)
    parts[z, Q:Q + 1] = jnp.sum(jnp.where(row == lane, squares, 0.0), axis=0, keepdims=True)
    for _, to in on_line():
        send(parts.at[z, sent_rows], parts.at[z, sent_rows], PC_, to)
    done(sf_all.at[pl.ds(0, NZ - 1)], SF_).wait_recv()
    self2 = sf_all[...].reshape(2 * G, 512)
    send(pooled, pool_in, PB_, partner)
    send(sf_all, self_in, SB_, partner)
    done(parts.at[pl.ds(0, NZ - 1), sent_rows], PC_).wait_recv()
    total, squares = parts[0, 0:Q], parts[0, Q:Q + 1]
    for f in range(1, NZ):
        total, squares = total + parts[f, 0:Q], squares + parts[f, Q:Q + 1]
    sums = jnp.concatenate(
        [total[:, (C - 1) * j:(C - 1) * (j + 1)] for j in range(NZ)], axis=0
    )
    squares = jnp.sum(
        jnp.where(row == lane, jnp.broadcast_to(squares, (G, L)), 0.0), axis=1, keepdims=True
    )
    norm = jnp.sqrt(squares + EPS)
    ahead = sums / norm
    slope = jax.nn.sigmoid(ahead + MARGIN)
    slope_sum = jnp.sum(slope, axis=1, keepdims=True)
    along = jnp.sum(slope * ahead, axis=1, keepdims=True)

    def coef(k):
        if k == 0:
            return jnp.broadcast_to(-slope_sum, (G, L))
        return spread(slope, k - 1)

    grad_unit = jnp.zeros((G, L), F32)
    for k in range(1, C):
        grad_unit = grad_unit + coef(k) * cand[k]
    unit = act / norm
    grad_act = (grad_unit - unit * along) / norm
    grad_pre = grad_act * gate * (1.0 + pre * (1.0 - gate))
    gp16 = grad_pre.astype(BF16)
    gp32 = gp16.astype(F32)

    def rows_of(part):
        return pl.ds(PARTS[part][0] * Q, (PARTS[part][1] - PARTS[part][0]) * Q)

    def spread_out(n, part):
        rows_at = rows_of(part)
        for other, to in on_face():
            send(face_out.at[n, other, rows_at], face_in.at[n, e, rows_at], FACE_ + 3 * n + part, to)

    def reduce_half(n, half_of):
        for k in range(NE):
            face_out[n, k] = half_of(k // NX, k % NX).reshape(NZ * Q, L).astype(BF16)
        face_in[n, e] = face_out[n, e]
        spread_out(n, 0)

    def both_cores(mine, theirs):
        return jnp.concatenate([mine, theirs], axis=0)

    def two_blocks(rows):
        blank = jnp.zeros((Q, L), F32)
        pieces = []
        for j in range(NZ):
            part = rows[j * Q:(j + 1) * Q].astype(F32)
            pieces.append(jnp.concatenate([part, blank], axis=1))
            pieces.append(jnp.concatenate([blank, part], axis=1))
        return jnp.concatenate(pieces, axis=0).astype(BF16)

    gx_out[0] = (gp32 * inv).astype(BF16)
    gx_out[1] = gp16
    gx_out[2] = unit.astype(BF16)
    send(gx_out, gx_in, GX_, partner)
    for m in range((C + 1) // 2):
        k = 2 * m
        last = zero if k + 1 == C else hit(ids_lo, K + k + 1, coef(k + 1))
        cand_lo[:, k * Q:(k + 2) * Q] = pair(hit(ids_lo, K + k, coef(k)), last)
    outer(w2, cand_hi, cand_lo)
    send(w2.at[:, away], w2_in, W2_, partner)
    done(hot_in, HP_).wait_recv()
    done(gx_in, GX_).wait_recv()

    rx[...] = tdot(
        both_cores(hot[0, :, half], hot_in[...]), both_cores(gx_out[0], gx_in[0])
    ).reshape(NZ, NY, NX, Q, L)
    reduce_half(0, lambda yy, xx: rx[:, yy, xx])

    done(pool_in, PB_).wait_recv()
    done(self_in, SB_).wait_recv()
    self_rows = both_cores(self2, self_in[...].reshape(2 * G, 512))
    gw_self = tdot(self_rows, both_cores(two_blocks(gp16), two_blocks(gx_in[1])))
    rw[0:2] = gw_self[:, :L].reshape(2, NY, 2, NX, Q, L)
    rw[2:4] = gw_self[:, L:].reshape(2, NY, 2, NX, Q, L)
    pool_both = both_cores(pool_all, jnp.concatenate([pool_in[f] for f in range(NZ)], axis=1))
    rw[4:8] = tdot(pool_both, both_cores(gp16, gx_in[1])).reshape(4, NY, 2, NX, Q, L)
    reduce_half(2, lambda yy, xx: rw[:, yy, c, xx])

    done(w2_in, W2_).wait_recv()
    ry[...] = tdot(
        both_cores(w2[:, half], w2_in[...]), both_cores(gx_out[2], gx_in[2])
    ).reshape(NZ, NY, NX, Q, L)
    reduce_half(1, lambda yy, xx: ry[:, yy, xx])

    gsend[...] = gp32.reshape(NZ, Q, L)
    for other, to in on_line():
        send(gsend.at[other], grecv.at[z], GP_, to)
    grecv[z] = gsend[z]
    for part in range(1, len(PARTS)):
        for n in (0, 2, 1):
            spread_out(n, part)

    done(grecv.at[pl.ds(0, NZ - 1)], GP_).wait_recv()
    gp_own = jnp.concatenate([grecv[f] for f in range(NZ)], axis=1).astype(BF16)
    o_self[...] = ntdot(gp_own, wtop[...])

    def finish(n, part):
        rows_at = rows_of(part)
        done(face_in.at[n, pl.ds(0, NE - 1), rows_at], FACE_ + 3 * n + part).wait_recv()
        acc = face_in[n, 0, rows_at].astype(F32)
        for k in range(1, NE):
            acc = acc + face_in[n, k, rows_at].astype(F32)
        first, end = PARTS[part]
        line_out[n, first:end] = acc.reshape(end - first, Q, L)
        for to_z in range(first, end):
            @pl.when(z == to_z)
            def _():
                line_in[n, to_z] = line_out[n, to_z]

            @pl.when(z != to_z)
            def _():
                send(line_out.at[n, to_z], line_in.at[n, z], LINE_ + n, ((to_z * NY + y) * 2 + c, x))

    def row_sums(n):
        done(line_in.at[n, pl.ds(0, NZ - 1)], LINE_ + n).wait_recv()
        return jnp.concatenate([line_in[n, f] for f in range(NZ)], axis=1)

    for part in range(len(PARTS)):
        for n in (0, 2, 1):
            finish(n, part)
    before = row_sums(0)
    rest = before - before.astype(BF16).astype(F32)
    loads[2].wait()
    after = ntdot(jnp.concatenate([before, rest], axis=0).astype(BF16), wbot[...])
    o_t[...] = after[0:Q] + after[Q:2 * Q] + row_sums(1)
    o_w[...] = row_sums(2)

    for ref, row in (
        (qi.at[pl.ds(0, NZ - 1)], QI_), (sf_all.at[pl.ds(0, NZ - 1)], SF_),
        (t_all.at[c], TP_), (pooled.at[pl.ds(0, NZ - 1)], PO_),
        (parts.at[pl.ds(0, NZ - 1), sent_rows], PC_), (gsend.at[pl.ds(0, NZ - 1)], GP_),
        (ps_out.at[pl.ds(0, NZ - 1)], PS_), (hot.at[0, :, away], HP_), (gx_out, GX_),
        (w2.at[:, away], W2_), (pooled, PB_), (sf_all, SB_),
    ):
        done(ref, row).wait_send()
    for k in range(NZ):
        if k:
            done(t_all.at[c, b], TZ_ + k).wait_send()
        done(t_all.at[c, pl.ds(0, NY - 1)], TY_ + k).wait_send()
    for n in range(3):
        for part in range(len(PARTS)):
            rows_at = rows_of(part)
            done(face_out.at[n, pl.ds(0, NE - 1), rows_at], FACE_ + 3 * n + part).wait_send()
        done(line_out.at[n, pl.ds(0, NZ - 1)], LINE_ + n).wait_send()


def hand_over(a, b, c, to_a, to_b, to_c):
    to_a[...] = a[...]
    to_b[...] = b[...]
    to_c[...] = c[...]


def local(table, self_feat, weight, owners, item_rows, importance):
    vmem = pl.BlockSpec(memory_space=pltpu.VMEM)
    hbm = pl.BlockSpec(memory_space=pl.ANY)
    out = jax.ShapeDtypeStruct((Q, 1024), F32)
    V = pltpu.VMEM
    grads = pl.pallas_call(
        kernel,
        out_shape=(out, out, out),
        in_specs=[hbm] * 6,
        out_specs=(vmem, vmem, vmem),
        scratch_shapes=[
            V((32, 1024), BF16),
            V((Q, 1024), BF16),
            V((Q, K + C), jnp.int32),
            V((Q, K + C), jnp.int32),
            V((Q, K), jnp.int32),
            V((2, NB, 32, L), BF16),
            V((NZ, Q, L), jnp.int32),
            V((NZ, 2 * Q, 512), BF16),
            V((NZ, Q, L), F32),
            V((NZ, Q, L), F32),
            V((NZ, G, L), BF16),
            V((NZ, 2 * Q, L), F32),
            V((NZ, Q, L), F32),
            V((NZ, Q, L), F32),
            V((1 + C, G, ITEMS), BF16),
            V((C, G, L), jnp.int32),
            V((C, G, L), F32),
            V((G, ITEMS), BF16),
            V((G, HALF), BF16),
            V((3, G, L), BF16),
            V((3, G, L), BF16),
            V((NZ, K * Q, L), BF16),
            V((NZ, K * Q, L), BF16),
            V((NZ, (C + 1) * Q, L), BF16),
            V((NZ, (C + 1) * Q, L), BF16),
            V((1024, L), BF16),
            V((1024, 1024), BF16),
            V((1024, 1024), BF16),
            V((NZ, NY, NX, Q, L), F32),
            V((NZ, NY, 2, NX, Q, L), F32),
            V((NZ, NY, NX, Q, L), F32),
            V((NZ, G, L), BF16),
            V((NZ, 2 * Q, 512), BF16),
            V((G, HALF), BF16),
            V((3, NE, G, L), BF16),
            V((3, NE, G, L), BF16),
            V((3, NZ, Q, L), F32),
            V((3, NZ, Q, L), F32),
            pltpu.SemaphoreType.DMA((40, 2)),
            pltpu.SemaphoreType.DMA((8,)),
        ],
        compiler_params=pltpu.CompilerParams(
            collective_id=0, has_side_effects=True, vmem_limit_bytes=62 * 1024 * 1024
        ),
    )(table, self_feat, owners.reshape(Q, K + C), item_rows, importance, weight)
    return pl.pallas_call(
        hand_over, out_shape=(out, out, out), in_specs=[vmem] * 3, out_specs=(vmem,) * 3
    )(*grads)


def solution(mesh):
    both = ("shard", "rep")
    in_specs = (
        P("shard", None), P(both, None), P(), P(both, None, None), P(both, None), P(both, None),
    )
    out_specs = (P(both, None), P(both, None), P(both, None))
    return jax.shard_map(local, mesh=mesh, in_specs=in_specs, out_specs=out_specs, check_vma=False)
```

```python
import jax
import jax.numpy as jnp
from jax import lax
from jax.experimental import pallas as pl
from jax.experimental.pallas import tpu as pltpu
from jax.sharding import PartitionSpec as P

MESH = pl.DeviceIdType.MESH
MARGIN = 0.5
EPS = 1e-06
K = 50
C = 17
NZ, NY, NX = 8, 4, 4
NB = NZ * NY
NE = NY * NX
Q = 8
G = NZ * Q
L = 128
ITEMS = 2048
HALF = ITEMS // 2
F32, BF16 = jnp.float32, jnp.bfloat16
PARTS = ((0, 4), (4, 8))
QI_, SF_, TP_, PO_, PC_, GP_, PS_, HP_, GX_, W2_, PB_, SB_ = range(12)
LINE_, FACE_ = 12, 15
TZ_, TY_ = 24, 32


def tdot(a, b):
    return lax.dot_general(a, b, (((0,), (0,)), ((), ())), preferred_element_type=F32)


def ntdot(a, b):
    return lax.dot_general(a, b, (((1,), (1,)), ((), ())), preferred_element_type=F32)


def kernel(
    tab_hbm, sf_hbm, own_hbm, row_hbm, imp_hbm, w_hbm, o_self, o_w, o_t,
    tab, sf, own_in, row_in, imp_in,
    t_all, qi, sf_all, ps_out, ps_in, pooled, parts, gsend, grecv, hot, id_b, cand, w2, hot_in, gx_out, gx_in,
    at_cand, at_hi, at_lo, cand_hi, cand_lo,
    wf, wtop, wbot, hot_t, self_t, pool_t, rx, rw, ry, pool_in, self_in, w2_in, face_out, face_in, line_out, line_in,
    sems, wsem,
):
    s = lax.axis_index("shard")
    x = lax.axis_index("rep")
    c = s & 1
    b = s >> 1
    z = b >> 2
    y = b & (NY - 1)
    e = y * NX + x
    partner = (b * 2 + 1 - c, x)

    def on_line():
        for k in (4, 3, 5, 2, 6, 1, 7):
            other = (z + k) & (NZ - 1)
            yield other, ((other * NY + y) * 2 + c, x)

    def on_face():
        steps = [(dy, dx) for dy in range(NY) for dx in range(NX)][1:]
        for dy, dx in sorted(steps, key=lambda step: -min(step[0], 4 - step[0]) - min(step[1], 4 - step[1])):
            yy, xx = (y + dy) & (NY - 1), (x + dx) & (NX - 1)
            yield yy * NX + xx, ((z * NY + yy) * 2 + c, xx)

    def send(src, dst, row, to):
        pltpu.make_async_remote_copy(
            src_ref=src, dst_ref=dst, send_sem=sems.at[row, 0], recv_sem=sems.at[row, 1],
            device_id=to, device_id_type=MESH,
        ).start()

    def done(ref, row):
        return pltpu.make_async_remote_copy(
            src_ref=ref, dst_ref=ref, send_sem=sems.at[row, 0], recv_sem=sems.at[row, 1],
            device_id=partner, device_id_type=MESH,
        )

    bar = pltpu.get_barrier_semaphore()

    def greet(to):
        pl.semaphore_signal(bar, inc=1, device_id=to, device_id_type=MESH)

    for _, to in [*on_line(), *on_face()]:
        greet(to)
    greet(partner)

    zcol = pl.ds(pl.multiple_of(z * L, L), L)
    loads = [
        pltpu.make_async_copy(w_hbm.at[pl.ds(1024, 1024), zcol], wf, wsem.at[0]),
        pltpu.make_async_copy(w_hbm.at[pl.ds(0, 1024), :], wtop, wsem.at[1]),
        pltpu.make_async_copy(w_hbm.at[pl.ds(1024, 1024), :], wbot, wsem.at[2]),
    ]
    small = [
        pltpu.make_async_copy(src, dst, wsem.at[3 + i])
        for i, (src, dst) in enumerate((
            (own_hbm, own_in), (row_hbm, row_in), (imp_hbm, imp_in), (tab_hbm, tab), (sf_hbm, sf)))
    ]
    for load in small + loads:
        load.start()

    small[3].wait()
    t_all[c, b] = tab[:, zcol]
    pl.semaphore_wait(bar, NZ - 1 + NE - 1 + 1)

    for k in (4, 3, 5, 2, 6, 1, 7):
        to_z = (z - k) & (NZ - 1)
        cols = pl.ds(pl.multiple_of(to_z * L, L), L)
        send(tab.at[:, cols], t_all.at[c, b], TZ_ + k, ((to_z * NY + y) * 2 + c, x))

    def pass_on(k):
        at = t_all.at[c, ((z + k) & (NZ - 1)) * NY + y]
        for dy in (2, 1, 3):
            send(at, at, TY_ + k, ((z * NY + ((y + dy) & (NY - 1))) * 2 + c, x))
        send(at, at, TP_, partner)

    pass_on(0)
    for load in small[:3]:
        load.wait()
    own = own_in[...]
    at = (own & 1) * HALF + (own >> 1) * 32 + row_in[...]
    qi[z] = jnp.zeros((Q, L), jnp.int32)
    qi[z, :, 0:K + C] = at
    qi[z, :, K + C:2 * K + C] = imp_in[...]
    for _, to in on_line():
        send(qi.at[z], qi.at[z], QI_, to)
    for k in (1, 7, 2, 6, 3, 5, 4):
        done(t_all.at[c, b], TZ_ + k).wait_recv()
        pass_on(k)

    small[4].wait()
    loads[1].wait()
    own_pre = jnp.dot(sf[...], wtop[...], preferred_element_type=F32)
    for f in range(NZ):
        ps_out[f] = own_pre[:, f * L:(f + 1) * L]
    for other, to in on_line():
        send(ps_out.at[other], ps_in.at[z], PS_, to)
    ps_in[z] = ps_out[z]
    own_self = sf[...].astype(F32)
    sf_all[z] = jnp.concatenate([own_self[:, :512], own_self[:, 512:]], axis=0).astype(BF16)
    for _, to in on_line():
        send(sf_all.at[z], sf_all.at[z], SF_, to)

    done(qi.at[pl.ds(0, NZ - 1)], QI_).wait_recv()
    ids = qi[...].reshape(G, L)
    imp = ids.astype(F32)
    lane = lax.broadcasted_iota(jnp.int32, (G, L), 1)
    query = lax.broadcasted_iota(jnp.int32, (G, L), 0) & (Q - 1)
    weighed = (lane >= K + C) & (lane < 2 * K + C)
    inv = 1.0 / jnp.sum(jnp.where(weighed, imp, 0.0), axis=1, keepdims=True)
    ids_hi = (ids >> 7) * Q + query
    ids_lo = ids & (L - 1)

    def spread(values, k):
        return jnp.broadcast_to(values[:, k:k + 1], (G, L))

    def pair(one, two):
        both = jnp.concatenate([one.reshape(NZ, Q, L), two.reshape(NZ, Q, L)], axis=1)
        return both.astype(BF16)

    def hit(values, k, weight=1.0):
        return jnp.where(spread(values, k) == lane, weight, 0.0)

    def outer(out, hi, lo):
        def block(m, carry):
            one = tdot(hi[2 * m], lo[2 * m])
            two = tdot(hi[2 * m + 1], lo[2 * m + 1])
            rows_at = pl.ds(pl.multiple_of(2 * m * Q, 2 * Q), 2 * Q)
            for h in range(ITEMS // L):
                both = jnp.concatenate([one[h * Q:(h + 1) * Q], two[h * Q:(h + 1) * Q]], axis=0)
                out[rows_at, h * L:(h + 1) * L] = both.astype(BF16)
            return carry

        lax.fori_loop(0, NZ // 2, block, 0)

    for m in range(K // 2):
        k = 2 * m
        at_hi[:, k * Q:(k + 2) * Q] = pair(hit(ids_hi, k), hit(ids_hi, k + 1))
        at_lo[:, k * Q:(k + 2) * Q] = pair(
            hit(ids_lo, k, spread(imp, K + C + k)), hit(ids_lo, k + 1, spread(imp, K + C + k + 1)))
    outer(hot.at[0], at_hi, at_lo)

    for k in (0, 1, 7, 2, 6, 3, 5, 4):
        first = ((z + k) & (NZ - 1)) * NY
        done(t_all.at[c, pl.ds(first, NY - 1)], TY_ + k).wait_recv()
        for dy in range(1, NY):
            at = t_all.at[c, first + ((y + dy) & (NY - 1))]
            send(at, at, TP_, partner)
    done(t_all.at[1 - c], TP_).wait_recv()

    rows = t_all[...].reshape(ITEMS, L)
    mine = jnp.dot(hot[0], rows, preferred_element_type=F32) * inv
    pooled[z] = mine.astype(BF16)
    for _, to in on_line():
        send(pooled.at[z], pooled.at[z], PO_, to)
    half = pl.ds(pl.multiple_of(c * HALF, HALF), HALF)
    away = pl.ds(pl.multiple_of((1 - c) * HALF, HALF), HALF)
    send(hot.at[0, :, away], hot_in, HP_, partner)
    for k in range(C):
        id_b[k] = spread(ids, K + k)

    def hot_chunk(h, carry):
        here = lane + h * L
        cols = pl.ds(pl.multiple_of(h * L, L), L)
        for k in range(C):
            hot[1 + k, :, cols] = jnp.where(id_b[k] == here, 1.0, 0.0).astype(BF16)
        return carry

    lax.fori_loop(0, ITEMS // L, hot_chunk, 0)
    cand[...] = jnp.dot(
        hot[1:1 + C].reshape(C * G, ITEMS), rows, preferred_element_type=F32
    ).reshape(C, G, L)
    for k in range(1, C):
        cand[k] = cand[k] - cand[0]

    zero = jnp.zeros((G, L), F32)
    for m in range((C + 1) // 2):
        k = K + 2 * m
        last = zero if 2 * m + 1 == C else hit(ids_hi, k + 1)
        cand_hi[:, 2 * m * Q:(2 * m + 2) * Q] = pair(hit(ids_hi, k), last)
    for k in range(C):
        at_cand[k] = hit(ids_lo, K + k)
    loads[0].wait()
    done(pooled.at[pl.ds(0, NZ - 1)], PO_).wait_recv()
    pool_all = jnp.concatenate([pooled[f] for f in range(NZ)], axis=1)
    done(ps_in.at[pl.ds(0, NZ - 1)], PS_).wait_recv()
    pre = ps_in[...].reshape(G, L) + jnp.dot(pool_all, wf[...], preferred_element_type=F32)
    gate = jax.nn.sigmoid(pre)
    act = pre * gate
    sent_rows = pl.ds(0, Q + 1)
    row = lax.broadcasted_iota(jnp.int32, (G, L), 0)
    where_at = lane - (C - 1) * (row >> 3)
    acc = zero
    for k in range(1, C):
        acc = jnp.where(where_at == k - 1, jnp.sum(act * cand[k], axis=1, keepdims=True), acc)
    parts[z, 0:Q] = jnp.sum(acc.reshape(NZ, Q, L), axis=0)
    squares = jnp.sum(act * act, axis=1, keepdims=True)
    parts[z, Q:Q + 1] = jnp.sum(jnp.where(row == lane, squares, 0.0), axis=0, keepdims=True)
    for _, to in on_line():
        send(parts.at[z, sent_rows], parts.at[z, sent_rows], PC_, to)
    def both_cores(mine, theirs):
        return jnp.concatenate([mine, theirs], axis=0)

    done(sf_all.at[pl.ds(0, NZ - 1)], SF_).wait_recv()
    self2 = sf_all[...].reshape(2 * G, 512)
    send(pooled, pool_in, PB_, partner)
    send(sf_all, self_in, SB_, partner)
    done(hot_in, HP_).wait_recv()
    hot_t[...] = both_cores(hot[0, :, half], hot_in[...]).T
    done(pool_in, PB_).wait_recv()
    done(self_in, SB_).wait_recv()
    self_t[...] = both_cores(self2, self_in[...].reshape(2 * G, 512)).T
    pool_t[...] = both_cores(
        pool_all, jnp.concatenate([pool_in[f] for f in range(NZ)], axis=1)).T
    done(parts.at[pl.ds(0, NZ - 1), sent_rows], PC_).wait_recv()
    total, squares = parts[0, 0:Q], parts[0, Q:Q + 1]
    for f in range(1, NZ):
        total, squares = total + parts[f, 0:Q], squares + parts[f, Q:Q + 1]
    sums = jnp.concatenate(
        [total[:, (C - 1) * j:(C - 1) * (j + 1)] for j in range(NZ)], axis=0
    )
    squares = jnp.sum(
        jnp.where(row == lane, jnp.broadcast_to(squares, (G, L)), 0.0), axis=1, keepdims=True
    )
    norm = jnp.sqrt(squares + EPS)
    ahead = sums / norm
    slope = jax.nn.sigmoid(ahead + MARGIN)
    slope_sum = jnp.sum(slope, axis=1, keepdims=True)
    along = jnp.sum(slope * ahead, axis=1, keepdims=True)

    def coef(k):
        if k == 0:
            return jnp.broadcast_to(-slope_sum, (G, L))
        return spread(slope, k - 1)

    grad_unit = jnp.zeros((G, L), F32)
    for k in range(1, C):
        grad_unit = grad_unit + coef(k) * cand[k]
    unit = act / norm
    grad_act = (grad_unit - unit * along) / norm
    grad_pre = grad_act * gate * (1.0 + pre * (1.0 - gate))
    gp16 = grad_pre.astype(BF16)
    gp32 = gp16.astype(F32)

    def rows_of(part):
        return pl.ds(PARTS[part][0] * Q, (PARTS[part][1] - PARTS[part][0]) * Q)

    def spread_out(n, part):
        rows_at = rows_of(part)
        for other, to in on_face():
            send(face_out.at[n, other, rows_at], face_in.at[n, e, rows_at], FACE_ + 3 * n + part, to)

    def reduce_half(n, half_of):
        for k in range(NE):
            face_out[n, k] = half_of(k // NX, k % NX).reshape(NZ * Q, L).astype(BF16)
        face_in[n, e] = face_out[n, e]
        spread_out(n, 0)

    def two_blocks(rows):
        blank = jnp.zeros((Q, L), F32)
        pieces = []
        for j in range(NZ):
            part = rows[j * Q:(j + 1) * Q].astype(F32)
            pieces.append(jnp.concatenate([part, blank], axis=1))
            pieces.append(jnp.concatenate([blank, part], axis=1))
        return jnp.concatenate(pieces, axis=0).astype(BF16)

    gx_out[0] = (gp32 * inv).astype(BF16)
    gx_out[1] = gp16
    gx_out[2] = unit.astype(BF16)
    send(gx_out, gx_in, GX_, partner)
    for m in range((C + 1) // 2):
        k = 2 * m
        last = zero if k + 1 == C else at_cand[k + 1] * coef(k + 1)
        cand_lo[:, k * Q:(k + 2) * Q] = pair(at_cand[k] * coef(k), last)
    outer(w2, cand_hi, cand_lo)
    send(w2.at[:, away], w2_in, W2_, partner)
    done(gx_in, GX_).wait_recv()

    rx[...] = jnp.dot(
        hot_t[...], both_cores(gx_out[0], gx_in[0]), preferred_element_type=F32
    ).reshape(NZ, NY, NX, Q, L)
    reduce_half(0, lambda yy, xx: rx[:, yy, xx])

    gw_self = jnp.dot(
        self_t[...], both_cores(two_blocks(gp16), two_blocks(gx_in[1])), preferred_element_type=F32)
    rw[0:2] = gw_self[:, :L].reshape(2, NY, 2, NX, Q, L)
    rw[2:4] = gw_self[:, L:].reshape(2, NY, 2, NX, Q, L)
    gw_pool = jnp.dot(pool_t[...], both_cores(gp16, gx_in[1]), preferred_element_type=F32)
    rw[4:8] = gw_pool.reshape(4, NY, 2, NX, Q, L)
    reduce_half(2, lambda yy, xx: rw[:, yy, c, xx])

    done(w2_in, W2_).wait_recv()
    ry[...] = tdot(
        both_cores(w2[:, half], w2_in[...]), both_cores(gx_out[2], gx_in[2])
    ).reshape(NZ, NY, NX, Q, L)
    reduce_half(1, lambda yy, xx: ry[:, yy, xx])

    gsend[...] = gp32.reshape(NZ, Q, L)
    for other, to in on_line():
        send(gsend.at[other], grecv.at[z], GP_, to)
    grecv[z] = gsend[z]
    for part in range(1, len(PARTS)):
        for n in (0, 2, 1):
            spread_out(n, part)

    done(grecv.at[pl.ds(0, NZ - 1)], GP_).wait_recv()
    gp_own = jnp.concatenate([grecv[f] for f in range(NZ)], axis=1).astype(BF16)
    o_self[...] = ntdot(gp_own, wtop[...])

    def finish(n, part):
        rows_at = rows_of(part)
        done(face_in.at[n, pl.ds(0, NE - 1), rows_at], FACE_ + 3 * n + part).wait_recv()
        acc = face_in[n, 0, rows_at].astype(F32)
        for k in range(1, NE):
            acc = acc + face_in[n, k, rows_at].astype(F32)
        first, end = PARTS[part]
        line_out[n, first:end] = acc.reshape(end - first, Q, L)
        for to_z in range(first, end):
            @pl.when(z == to_z)
            def _():
                line_in[n, to_z] = line_out[n, to_z]

            @pl.when(z != to_z)
            def _():
                send(line_out.at[n, to_z], line_in.at[n, z], LINE_ + n, ((to_z * NY + y) * 2 + c, x))

    def row_sums(n):
        done(line_in.at[n, pl.ds(0, NZ - 1)], LINE_ + n).wait_recv()
        return jnp.concatenate([line_in[n, f] for f in range(NZ)], axis=1)

    for part in range(len(PARTS)):
        for n in (0, 2, 1):
            finish(n, part)
    before = row_sums(0)
    rest = before - before.astype(BF16).astype(F32)
    loads[2].wait()
    after = ntdot(jnp.concatenate([before, rest], axis=0).astype(BF16), wbot[...])
    o_t[...] = after[0:Q] + after[Q:2 * Q] + row_sums(1)
    o_w[...] = row_sums(2)

    for ref, row in (
        (qi.at[pl.ds(0, NZ - 1)], QI_), (sf_all.at[pl.ds(0, NZ - 1)], SF_),
        (t_all.at[c], TP_), (pooled.at[pl.ds(0, NZ - 1)], PO_),
        (parts.at[pl.ds(0, NZ - 1), sent_rows], PC_), (gsend.at[pl.ds(0, NZ - 1)], GP_),
        (ps_out.at[pl.ds(0, NZ - 1)], PS_), (hot.at[0, :, away], HP_), (gx_out, GX_),
        (w2.at[:, away], W2_), (pooled, PB_), (sf_all, SB_),
    ):
        done(ref, row).wait_send()
    for k in range(NZ):
        if k:
            done(t_all.at[c, b], TZ_ + k).wait_send()
        done(t_all.at[c, pl.ds(0, NY - 1)], TY_ + k).wait_send()
    for n in range(3):
        for part in range(len(PARTS)):
            rows_at = rows_of(part)
            done(face_out.at[n, pl.ds(0, NE - 1), rows_at], FACE_ + 3 * n + part).wait_send()
        done(line_out.at[n, pl.ds(0, NZ - 1)], LINE_ + n).wait_send()


def hand_over(a, b, c, to_a, to_b, to_c):
    to_a[...] = a[...]
    to_b[...] = b[...]
    to_c[...] = c[...]


def local(table, self_feat, weight, owners, item_rows, importance):
    vmem = pl.BlockSpec(memory_space=pltpu.VMEM)
    hbm = pl.BlockSpec(memory_space=pl.ANY)
    out = jax.ShapeDtypeStruct((Q, 1024), F32)
    V = pltpu.VMEM
    grads = pl.pallas_call(
        kernel,
        out_shape=(out, out, out),
        in_specs=[hbm] * 6,
        out_specs=(vmem, vmem, vmem),
        scratch_shapes=[
            V((32, 1024), BF16),
            V((Q, 1024), BF16),
            V((Q, K + C), jnp.int32),
            V((Q, K + C), jnp.int32),
            V((Q, K), jnp.int32),
            V((2, NB, 32, L), BF16),
            V((NZ, Q, L), jnp.int32),
            V((NZ, 2 * Q, 512), BF16),
            V((NZ, Q, L), F32),
            V((NZ, Q, L), F32),
            V((NZ, G, L), BF16),
            V((NZ, 2 * Q, L), F32),
            V((NZ, Q, L), F32),
            V((NZ, Q, L), F32),
            V((1 + C, G, ITEMS), BF16),
            V((C, G, L), jnp.int32),
            V((C, G, L), F32),
            V((G, ITEMS), BF16),
            V((G, HALF), BF16),
            V((3, G, L), BF16),
            V((3, G, L), BF16),
            V((C, G, L), F32),
            V((NZ, K * Q, L), BF16),
            V((NZ, K * Q, L), BF16),
            V((NZ, (C + 1) * Q, L), BF16),
            V((NZ, (C + 1) * Q, L), BF16),
            V((1024, L), BF16),
            V((1024, 1024), BF16),
            V((1024, 1024), BF16),
            V((HALF, 2 * G), BF16),
            V((512, 4 * G), BF16),
            V((1024, 2 * G), BF16),
            V((NZ, NY, NX, Q, L), F32),
            V((NZ, NY, 2, NX, Q, L), F32),
            V((NZ, NY, NX, Q, L), F32),
            V((NZ, G, L), BF16),
            V((NZ, 2 * Q, 512), BF16),
            V((G, HALF), BF16),
            V((3, NE, G, L), BF16),
            V((3, NE, G, L), BF16),
            V((3, NZ, Q, L), F32),
            V((3, NZ, Q, L), F32),
            pltpu.SemaphoreType.DMA((40, 2)),
            pltpu.SemaphoreType.DMA((8,)),
        ],
        compiler_params=pltpu.CompilerParams(
            collective_id=0, has_side_effects=True, vmem_limit_bytes=62 * 1024 * 1024
        ),
    )(table, self_feat, owners.reshape(Q, K + C), item_rows, importance, weight)
    return pl.pallas_call(
        hand_over, out_shape=(out, out, out), in_specs=[vmem] * 3, out_specs=(vmem,) * 3
    )(*grads)


def solution(mesh):
    both = ("shard", "rep")
    in_specs = (
        P("shard", None), P(both, None), P(), P(both, None, None), P(both, None), P(both, None),
    )
    out_specs = (P(both, None), P(both, None), P(both, None))
    return jax.shard_map(local, mesh=mesh, in_specs=in_specs, out_specs=out_specs, check_vma=False)
```

```python
import jax
import jax.numpy as jnp
from jax import lax
from jax.experimental import pallas as pl
from jax.experimental.pallas import tpu as pltpu
from jax.sharding import PartitionSpec as P

MESH = pl.DeviceIdType.MESH
MARGIN = 0.5
EPS = 1e-06
K = 50
C = 17
NZ, NY, NX = 8, 4, 4
NB = NZ * NY
NE = NY * NX
Q = 8
G = NZ * Q
L = 128
ITEMS = 2048
HALF = ITEMS // 2
F32, BF16 = jnp.float32, jnp.bfloat16
PARTS = ((0, 4), (4, 8))
QI_, SF_, TP_, PO_, PC_, GP_, PS_, HP_, GX_, W2_, PB_, SB_ = range(12)
LINE_, FACE_ = 12, 15
TZ_, TY_ = 24, 32


def tdot(a, b):
    return lax.dot_general(a, b, (((0,), (0,)), ((), ())), preferred_element_type=F32)


def ntdot(a, b):
    return lax.dot_general(a, b, (((1,), (1,)), ((), ())), preferred_element_type=F32)


def kernel(
    tab_hbm, sf_hbm, own_hbm, row_hbm, imp_hbm, w_hbm, o_self, o_w, o_t,
    tab, sf, own_in, row_in, imp_in,
    t_all, qi, sf_all, ps_out, ps_in, pooled, parts, gsend, grecv, hot, id_b, cand, w2, hot_in, gx_out, gx_in,
    at_cand, at_hi, at_lo, cand_hi, cand_lo,
    wf, wtop, wbot, hot_t, self_t, pool_t, rx, rw, ry, pool_in, self_in, w2_in, face_out, face_in, line_out, line_in,
    sems, wsem,
):
    s = lax.axis_index("shard")
    x = lax.axis_index("rep")
    c = s & 1
    b = s >> 1
    z = b >> 2
    y = b & (NY - 1)
    e = y * NX + x
    partner = (b * 2 + 1 - c, x)

    def on_line():
        for k in (4, 3, 5, 2, 6, 1, 7):
            other = (z + k) & (NZ - 1)
            yield other, ((other * NY + y) * 2 + c, x)

    def on_face():
        steps = [(dy, dx) for dy in range(NY) for dx in range(NX)][1:]
        for dy, dx in sorted(steps, key=lambda step: -min(step[0], 4 - step[0]) - min(step[1], 4 - step[1])):
            yy, xx = (y + dy) & (NY - 1), (x + dx) & (NX - 1)
            yield yy * NX + xx, ((z * NY + yy) * 2 + c, xx)

    def send(src, dst, row, to):
        pltpu.make_async_remote_copy(
            src_ref=src, dst_ref=dst, send_sem=sems.at[row, 0], recv_sem=sems.at[row, 1],
            device_id=to, device_id_type=MESH,
        ).start()

    def done(ref, row):
        return pltpu.make_async_remote_copy(
            src_ref=ref, dst_ref=ref, send_sem=sems.at[row, 0], recv_sem=sems.at[row, 1],
            device_id=partner, device_id_type=MESH,
        )

    bar = pltpu.get_barrier_semaphore()

    def greet(to):
        pl.semaphore_signal(bar, inc=1, device_id=to, device_id_type=MESH)

    for _, to in [*on_line(), *on_face()]:
        greet(to)
    greet(partner)

    zcol = pl.ds(pl.multiple_of(z * L, L), L)
    loads = [
        pltpu.make_async_copy(w_hbm.at[pl.ds(1024, 1024), zcol], wf, wsem.at[0]),
        pltpu.make_async_copy(w_hbm.at[pl.ds(0, 1024), :], wtop, wsem.at[1]),
        pltpu.make_async_copy(w_hbm.at[pl.ds(1024, 1024), :], wbot, wsem.at[2]),
    ]
    small = [
        pltpu.make_async_copy(src, dst, wsem.at[3 + i])
        for i, (src, dst) in enumerate((
            (own_hbm, own_in), (row_hbm, row_in), (imp_hbm, imp_in), (tab_hbm, tab), (sf_hbm, sf)))
    ]
    for load in small + loads:
        load.start()

    small[3].wait()
    t_all[c, b] = tab[:, zcol]
    pl.semaphore_wait(bar, NZ - 1 + NE - 1 + 1)

    for k in (4, 3, 5, 2, 6, 1, 7):
        to_z = (z - k) & (NZ - 1)
        cols = pl.ds(pl.multiple_of(to_z * L, L), L)
        send(tab.at[:, cols], t_all.at[c, b], TZ_ + k, ((to_z * NY + y) * 2 + c, x))

    def pass_on(k):
        at = t_all.at[c, ((z + k) & (NZ - 1)) * NY + y]
        for dy in (2, 1, 3):
            send(at, at, TY_ + k, ((z * NY + ((y + dy) & (NY - 1))) * 2 + c, x))
        send(at, at, TP_, partner)

    pass_on(0)
    for load in small[:3]:
        load.wait()
    own = own_in[...]
    at = (own & 1) * HALF + (own >> 1) * 32 + row_in[...]
    qi[z] = jnp.zeros((Q, L), jnp.int32)
    qi[z, :, 0:K + C] = at
    qi[z, :, K + C:2 * K + C] = imp_in[...]
    for _, to in on_line():
        send(qi.at[z], qi.at[z], QI_, to)
    for k in (1, 7, 2, 6, 3, 5, 4):
        done(t_all.at[c, b], TZ_ + k).wait_recv()
        pass_on(k)

    small[4].wait()
    loads[1].wait()
    own_pre = jnp.dot(sf[...], wtop[...], preferred_element_type=F32)
    for f in range(NZ):
        ps_out[f] = own_pre[:, f * L:(f + 1) * L]
    for other, to in on_line():
        send(ps_out.at[other], ps_in.at[z], PS_, to)
    ps_in[z] = ps_out[z]
    own_self = sf[...].astype(F32)
    sf_all[z] = jnp.concatenate([own_self[:, :512], own_self[:, 512:]], axis=0).astype(BF16)
    for _, to in on_line():
        send(sf_all.at[z], sf_all.at[z], SF_, to)

    done(qi.at[pl.ds(0, NZ - 1)], QI_).wait_recv()
    ids = qi[...].reshape(G, L)
    imp = ids.astype(F32)
    lane = lax.broadcasted_iota(jnp.int32, (G, L), 1)
    query = lax.broadcasted_iota(jnp.int32, (G, L), 0) & (Q - 1)
    weighed = (lane >= K + C) & (lane < 2 * K + C)
    inv = 1.0 / jnp.sum(jnp.where(weighed, imp, 0.0), axis=1, keepdims=True)
    ids_hi = (ids >> 7) * Q + query
    ids_lo = ids & (L - 1)

    def spread(values, k):
        return jnp.broadcast_to(values[:, k:k + 1], (G, L))

    def pair(one, two):
        both = jnp.concatenate([one.reshape(NZ, Q, L), two.reshape(NZ, Q, L)], axis=1)
        return both.astype(BF16)

    def hit(values, k, weight=1.0):
        return jnp.where(spread(values, k) == lane, weight, 0.0)

    def outer(out, hi, lo):
        def block(m, carry):
            one = tdot(hi[2 * m], lo[2 * m])
            two = tdot(hi[2 * m + 1], lo[2 * m + 1])
            rows_at = pl.ds(pl.multiple_of(2 * m * Q, 2 * Q), 2 * Q)
            for h in range(ITEMS // L):
                both = jnp.concatenate([one[h * Q:(h + 1) * Q], two[h * Q:(h + 1) * Q]], axis=0)
                out[rows_at, h * L:(h + 1) * L] = both.astype(BF16)
            return carry

        lax.fori_loop(0, NZ // 2, block, 0)

    for m in range(K // 2):
        k = 2 * m
        at_hi[:, k * Q:(k + 2) * Q] = pair(hit(ids_hi, k), hit(ids_hi, k + 1))
        at_lo[:, k * Q:(k + 2) * Q] = pair(
            hit(ids_lo, k, spread(imp, K + C + k)), hit(ids_lo, k + 1, spread(imp, K + C + k + 1)))
    outer(hot.at[0], at_hi, at_lo)

    for k in (0, 1, 7, 2, 6, 3, 5, 4):
        first = ((z + k) & (NZ - 1)) * NY
        done(t_all.at[c, pl.ds(first, NY - 1)], TY_ + k).wait_recv()
        for dy in range(1, NY):
            at = t_all.at[c, first + ((y + dy) & (NY - 1))]
            send(at, at, TP_, partner)
    half = pl.ds(pl.multiple_of(c * HALF, HALF), HALF)
    away = pl.ds(pl.multiple_of((1 - c) * HALF, HALF), HALF)
    near = jnp.dot(hot[0, :, half], t_all[c].reshape(HALF, L), preferred_element_type=F32)
    done(t_all.at[1 - c], TP_).wait_recv()
    far = jnp.dot(hot[0, :, away], t_all[1 - c].reshape(HALF, L), preferred_element_type=F32)
    mine = (near + far) * inv
    pooled[z] = mine.astype(BF16)
    for _, to in on_line():
        send(pooled.at[z], pooled.at[z], PO_, to)
    rows = t_all[...].reshape(ITEMS, L)
    send(hot.at[0, :, away], hot_in, HP_, partner)
    for k in range(C):
        id_b[k] = spread(ids, K + k)

    def hot_chunk(h, carry):
        here = lane + h * L
        cols = pl.ds(pl.multiple_of(h * L, L), L)
        for k in range(C):
            hot[1 + k, :, cols] = jnp.where(id_b[k] == here, 1.0, 0.0).astype(BF16)
        return carry

    lax.fori_loop(0, ITEMS // L, hot_chunk, 0)
    cand[...] = jnp.dot(
        hot[1:1 + C].reshape(C * G, ITEMS), rows, preferred_element_type=F32
    ).reshape(C, G, L)
    for k in range(1, C):
        cand[k] = cand[k] - cand[0]

    zero = jnp.zeros((G, L), F32)
    for m in range((C + 1) // 2):
        k = K + 2 * m
        last = zero if 2 * m + 1 == C else hit(ids_hi, k + 1)
        cand_hi[:, 2 * m * Q:(2 * m + 2) * Q] = pair(hit(ids_hi, k), last)
    for k in range(C):
        at_cand[k] = hit(ids_lo, K + k)
    loads[0].wait()
    done(pooled.at[pl.ds(0, NZ - 1)], PO_).wait_recv()
    pool_all = jnp.concatenate([pooled[f] for f in range(NZ)], axis=1)
    done(ps_in.at[pl.ds(0, NZ - 1)], PS_).wait_recv()
    pre = ps_in[...].reshape(G, L) + jnp.dot(pool_all, wf[...], preferred_element_type=F32)
    gate = jax.nn.sigmoid(pre)
    act = pre * gate
    sent_rows = pl.ds(0, Q + 1)
    row = lax.broadcasted_iota(jnp.int32, (G, L), 0)
    where_at = lane - (C - 1) * (row >> 3)
    acc = zero
    for k in range(1, C):
        acc = jnp.where(where_at == k - 1, jnp.sum(act * cand[k], axis=1, keepdims=True), acc)
    parts[z, 0:Q] = jnp.sum(acc.reshape(NZ, Q, L), axis=0)
    squares = jnp.sum(act * act, axis=1, keepdims=True)
    parts[z, Q:Q + 1] = jnp.sum(jnp.where(row == lane, squares, 0.0), axis=0, keepdims=True)
    for _, to in on_line():
        send(parts.at[z, sent_rows], parts.at[z, sent_rows], PC_, to)
    def both_cores(mine, theirs):
        return jnp.concatenate([mine, theirs], axis=0)

    done(sf_all.at[pl.ds(0, NZ - 1)], SF_).wait_recv()
    self2 = sf_all[...].reshape(2 * G, 512)
    send(pooled, pool_in, PB_, partner)
    send(sf_all, self_in, SB_, partner)
    done(hot_in, HP_).wait_recv()
    hot_t[...] = both_cores(hot[0, :, half], hot_in[...]).T
    done(pool_in, PB_).wait_recv()
    done(self_in, SB_).wait_recv()
    self_t[...] = both_cores(self2, self_in[...].reshape(2 * G, 512)).T
    pool_t[...] = both_cores(
        pool_all, jnp.concatenate([pool_in[f] for f in range(NZ)], axis=1)).T
    done(parts.at[pl.ds(0, NZ - 1), sent_rows], PC_).wait_recv()
    total, squares = parts[0, 0:Q], parts[0, Q:Q + 1]
    for f in range(1, NZ):
        total, squares = total + parts[f, 0:Q], squares + parts[f, Q:Q + 1]
    sums = jnp.concatenate(
        [total[:, (C - 1) * j:(C - 1) * (j + 1)] for j in range(NZ)], axis=0
    )
    squares = jnp.sum(
        jnp.where(row == lane, jnp.broadcast_to(squares, (G, L)), 0.0), axis=1, keepdims=True
    )
    norm = jnp.sqrt(squares + EPS)
    ahead = sums / norm
    slope = jax.nn.sigmoid(ahead + MARGIN)
    slope_sum = jnp.sum(slope, axis=1, keepdims=True)
    along = jnp.sum(slope * ahead, axis=1, keepdims=True)

    def coef(k):
        if k == 0:
            return jnp.broadcast_to(-slope_sum, (G, L))
        return spread(slope, k - 1)

    grad_unit = jnp.zeros((G, L), F32)
    for k in range(1, C):
        grad_unit = grad_unit + coef(k) * cand[k]
    unit = act / norm
    grad_act = (grad_unit - unit * along) / norm
    grad_pre = grad_act * gate * (1.0 + pre * (1.0 - gate))
    gp16 = grad_pre.astype(BF16)
    gp32 = gp16.astype(F32)

    def rows_of(part):
        return pl.ds(PARTS[part][0] * Q, (PARTS[part][1] - PARTS[part][0]) * Q)

    def spread_out(n, part):
        rows_at = rows_of(part)
        for other, to in on_face():
            send(face_out.at[n, other, rows_at], face_in.at[n, e, rows_at], FACE_ + 3 * n + part, to)

    def reduce_half(n, half_of):
        for k in range(NE):
            face_out[n, k] = half_of(k // NX, k % NX).reshape(NZ * Q, L).astype(BF16)
        face_in[n, e] = face_out[n, e]
        spread_out(n, 0)

    def two_blocks(rows):
        blank = jnp.zeros((Q, L), F32)
        pieces = []
        for j in range(NZ):
            part = rows[j * Q:(j + 1) * Q].astype(F32)
            pieces.append(jnp.concatenate([part, blank], axis=1))
            pieces.append(jnp.concatenate([blank, part], axis=1))
        return jnp.concatenate(pieces, axis=0).astype(BF16)

    gx_out[0] = (gp32 * inv).astype(BF16)
    gx_out[1] = gp16
    gx_out[2] = unit.astype(BF16)
    send(gx_out, gx_in, GX_, partner)
    for m in range((C + 1) // 2):
        k = 2 * m
        last = zero if k + 1 == C else at_cand[k + 1] * coef(k + 1)
        cand_lo[:, k * Q:(k + 2) * Q] = pair(at_cand[k] * coef(k), last)
    outer(w2, cand_hi, cand_lo)
    send(w2.at[:, away], w2_in, W2_, partner)
    done(gx_in, GX_).wait_recv()

    rx[...] = jnp.dot(
        hot_t[...], both_cores(gx_out[0], gx_in[0]), preferred_element_type=F32
    ).reshape(NZ, NY, NX, Q, L)
    reduce_half(0, lambda yy, xx: rx[:, yy, xx])

    gw_self = jnp.dot(
        self_t[...], both_cores(two_blocks(gp16), two_blocks(gx_in[1])), preferred_element_type=F32)
    rw[0:2] = gw_self[:, :L].reshape(2, NY, 2, NX, Q, L)
    rw[2:4] = gw_self[:, L:].reshape(2, NY, 2, NX, Q, L)
    gw_pool = jnp.dot(pool_t[...], both_cores(gp16, gx_in[1]), preferred_element_type=F32)
    rw[4:8] = gw_pool.reshape(4, NY, 2, NX, Q, L)
    reduce_half(2, lambda yy, xx: rw[:, yy, c, xx])

    done(w2_in, W2_).wait_recv()
    ry[...] = tdot(
        both_cores(w2[:, half], w2_in[...]), both_cores(gx_out[2], gx_in[2])
    ).reshape(NZ, NY, NX, Q, L)
    reduce_half(1, lambda yy, xx: ry[:, yy, xx])

    gsend[...] = gp32.reshape(NZ, Q, L)
    for other, to in on_line():
        send(gsend.at[other], grecv.at[z], GP_, to)
    grecv[z] = gsend[z]
    for part in range(1, len(PARTS)):
        for n in (0, 2, 1):
            spread_out(n, part)

    done(grecv.at[pl.ds(0, NZ - 1)], GP_).wait_recv()
    gp_own = jnp.concatenate([grecv[f] for f in range(NZ)], axis=1).astype(BF16)
    o_self[...] = ntdot(gp_own, wtop[...])

    def finish(n, part):
        rows_at = rows_of(part)
        done(face_in.at[n, pl.ds(0, NE - 1), rows_at], FACE_ + 3 * n + part).wait_recv()
        acc = face_in[n, 0, rows_at].astype(F32)
        for k in range(1, NE):
            acc = acc + face_in[n, k, rows_at].astype(F32)
        first, end = PARTS[part]
        line_out[n, first:end] = acc.reshape(end - first, Q, L)
        for to_z in range(first, end):
            @pl.when(z == to_z)
            def _():
                line_in[n, to_z] = line_out[n, to_z]

            @pl.when(z != to_z)
            def _():
                send(line_out.at[n, to_z], line_in.at[n, z], LINE_ + n, ((to_z * NY + y) * 2 + c, x))

    def row_sums(n):
        done(line_in.at[n, pl.ds(0, NZ - 1)], LINE_ + n).wait_recv()
        return jnp.concatenate([line_in[n, f] for f in range(NZ)], axis=1)

    for part in range(len(PARTS)):
        for n in (0, 2, 1):
            finish(n, part)
    before = row_sums(0)
    rest = before - before.astype(BF16).astype(F32)
    loads[2].wait()
    after = ntdot(jnp.concatenate([before, rest], axis=0).astype(BF16), wbot[...])
    o_t[...] = after[0:Q] + after[Q:2 * Q] + row_sums(1)
    o_w[...] = row_sums(2)

    for ref, row in (
        (qi.at[pl.ds(0, NZ - 1)], QI_), (sf_all.at[pl.ds(0, NZ - 1)], SF_),
        (t_all.at[c], TP_), (pooled.at[pl.ds(0, NZ - 1)], PO_),
        (parts.at[pl.ds(0, NZ - 1), sent_rows], PC_), (gsend.at[pl.ds(0, NZ - 1)], GP_),
        (ps_out.at[pl.ds(0, NZ - 1)], PS_), (hot.at[0, :, away], HP_), (gx_out, GX_),
        (w2.at[:, away], W2_), (pooled, PB_), (sf_all, SB_),
    ):
        done(ref, row).wait_send()
    for k in range(NZ):
        if k:
            done(t_all.at[c, b], TZ_ + k).wait_send()
        done(t_all.at[c, pl.ds(0, NY - 1)], TY_ + k).wait_send()
    for n in range(3):
        for part in range(len(PARTS)):
            rows_at = rows_of(part)
            done(face_out.at[n, pl.ds(0, NE - 1), rows_at], FACE_ + 3 * n + part).wait_send()
        done(line_out.at[n, pl.ds(0, NZ - 1)], LINE_ + n).wait_send()


def hand_over(a, b, c, to_a, to_b, to_c):
    to_a[...] = a[...]
    to_b[...] = b[...]
    to_c[...] = c[...]


def local(table, self_feat, weight, owners, item_rows, importance):
    vmem = pl.BlockSpec(memory_space=pltpu.VMEM)
    hbm = pl.BlockSpec(memory_space=pl.ANY)
    out = jax.ShapeDtypeStruct((Q, 1024), F32)
    V = pltpu.VMEM
    grads = pl.pallas_call(
        kernel,
        out_shape=(out, out, out),
        in_specs=[hbm] * 6,
        out_specs=(vmem, vmem, vmem),
        scratch_shapes=[
            V((32, 1024), BF16),
            V((Q, 1024), BF16),
            V((Q, K + C), jnp.int32),
            V((Q, K + C), jnp.int32),
            V((Q, K), jnp.int32),
            V((2, NB, 32, L), BF16),
            V((NZ, Q, L), jnp.int32),
            V((NZ, 2 * Q, 512), BF16),
            V((NZ, Q, L), F32),
            V((NZ, Q, L), F32),
            V((NZ, G, L), BF16),
            V((NZ, 2 * Q, L), F32),
            V((NZ, Q, L), F32),
            V((NZ, Q, L), F32),
            V((1 + C, G, ITEMS), BF16),
            V((C, G, L), jnp.int32),
            V((C, G, L), F32),
            V((G, ITEMS), BF16),
            V((G, HALF), BF16),
            V((3, G, L), BF16),
            V((3, G, L), BF16),
            V((C, G, L), F32),
            V((NZ, K * Q, L), BF16),
            V((NZ, K * Q, L), BF16),
            V((NZ, (C + 1) * Q, L), BF16),
            V((NZ, (C + 1) * Q, L), BF16),
            V((1024, L), BF16),
            V((1024, 1024), BF16),
            V((1024, 1024), BF16),
            V((HALF, 2 * G), BF16),
            V((512, 4 * G), BF16),
            V((1024, 2 * G), BF16),
            V((NZ, NY, NX, Q, L), F32),
            V((NZ, NY, 2, NX, Q, L), F32),
            V((NZ, NY, NX, Q, L), F32),
            V((NZ, G, L), BF16),
            V((NZ, 2 * Q, 512), BF16),
            V((G, HALF), BF16),
            V((3, NE, G, L), BF16),
            V((3, NE, G, L), BF16),
            V((3, NZ, Q, L), F32),
            V((3, NZ, Q, L), F32),
            pltpu.SemaphoreType.DMA((40, 2)),
            pltpu.SemaphoreType.DMA((8,)),
        ],
        compiler_params=pltpu.CompilerParams(
            collective_id=0, has_side_effects=True, vmem_limit_bytes=62 * 1024 * 1024
        ),
    )(table, self_feat, owners.reshape(Q, K + C), item_rows, importance, weight)
    return pl.pallas_call(
        hand_over, out_shape=(out, out, out), in_specs=[vmem] * 3, out_specs=(vmem,) * 3
    )(*grads)


def solution(mesh):
    both = ("shard", "rep")
    in_specs = (
        P("shard", None), P(both, None), P(), P(both, None, None), P(both, None), P(both, None),
    )
    out_specs = (P(both, None), P(both, None), P(both, None))
    return jax.shard_map(local, mesh=mesh, in_specs=in_specs, out_specs=out_specs, check_vma=False)
```
